512 devices in a mesh: seq: 64 (over z, y), head: 4 (over x), dp: 2 (over core).
Axes of the slice: x: 4, y: 4, z: 16, core: 2. Of those that a mesh axis runs over, the one named last changes fastest.
Arguments:
- queries: bfloat16 [2, 8192, 4096], P('dp', 'seq', 'head'), may hold values from -0.23925781 to 0.23925781
- key_rows: bfloat16 [2, 8192, 4096], P('dp', 'seq', 'head'), may hold values from -0.23925781 to 0.23925781
- values: bfloat16 [2, 8192, 4096], P('dp', 'seq', 'head'), may hold values from -6 to 6
- out_grad: bfloat16 [2, 8192, 4096], P('dp', 'seq', 'head'), may hold values from -6 to 6
- decay_rate: float32 [32], P('head'), may hold values from 4e-05 to 0.025, as said below
- rotation: float32 [4, 4096], P(None, 'head')
- refusal: float32 [4096, 2], P('head')
- proj_weight: float32 [4, 4096], P(None, 'head'), may hold values from -0.09375 to 0.09375
- proj_bias: float32 [4], replicated, may hold values from -4 to 4
- positions: int32 [2, 16], P('dp'), may hold values from 0 to 8191, as said below
Outputs:
- attended: bfloat16 [2, 8192, 4096], P('dp', 'seq', 'head')
- grad_query: bfloat16 [2, 8192, 4096], P('dp', 'seq', 'head')
- grad_key: bfloat16 [2, 8192, 4096], P('dp', 'seq', 'head')
- grad_value: bfloat16 [2, 8192, 4096], P('dp', 'seq', 'head')
- grad_rotation: float32 [4, 4096], P(None, 'head')
- grad_weight: float32 [4, 4096], P(None, 'head')
- grad_bias: float32 [4], replicated
The draws below stay inside these ranges and needn't reach their ends.
Inputs may be any that keep to these rules, and one draw needn't show every extreme that they name: 16 distinct positions in ascending order; among them always 0, 4096 and 8191. `decay_rate`: one rate per head, the same at every position.
All inputs are finite; a program needn't handle non-finite values.
Results may differ from the reference program's by a relative error of at most 0.0032.
Values sent between devices are 32-bit elements; how exact they have to be, the bound alone decides.
No kernel may reach another device: no remote copies, remote signals or barrier semaphores. Data moves between devices by JAX's collectives and lax.ppermute only.
A program may use at most 128 MiB of HBM per device.

```python
import math
import jax
import jax.numpy as jnp
from jax import lax

HEADS = 32
HDIM = 128
RANK = 4
REFUSE = 2
NPOS = 16
GROUP = 128
DOCS = 2
LENGTH = 8192
WIDTH = 4096


def shared_maps(key):
    first, second, third = jax.random.split(jax.random.fold_in(key, 17), 3)
    rotation = jax.random.normal(first, (RANK, WIDTH), jnp.float32) / math.sqrt(WIDTH)
    mixing = jax.random.normal(second, (RANK, REFUSE), jnp.float32) / math.sqrt(RANK)
    noise = jax.random.normal(third, (WIDTH, REFUSE), jnp.float32) / math.sqrt(WIDTH)
    blended = jnp.sum(rotation.T[:, :, None] * mixing[None, :, :], axis=1)
    return (rotation, 0.8 * blended + 0.6 * noise)


def draw_rotation(key, part):
    return shared_maps(key)[0]


def draw_refusal(key, part):
    return shared_maps(key)[1]


def draw_decay_rate(key, part):
    uniform_draw = jax.random.uniform(jax.random.fold_in(key, 3), (HEADS,), jnp.float32)
    lowest, highest_rate = (math.log(0.0001), math.log(0.025))
    return jnp.exp(lowest + uniform_draw * (highest_rate - lowest))


def draw_positions(key, part):
    half = LENGTH // 2

    def one_document(document_key):
        middle = jax.random.permutation(document_key, LENGTH - 3)[:NPOS - 3].astype(jnp.int32) + 1
        middle = jnp.where(middle >= half, middle + 1, middle)
        fixed = jnp.array([0, half, LENGTH - 1], jnp.int32)
        return jnp.sort(jnp.concatenate([fixed, middle]))
    document_keys = jax.random.split(jax.random.fold_in(key, 5), DOCS)
    return jax.vmap(one_document)(document_keys)


def shard_levels(rng, extent, cuts, smallest, top_value):
    gain, own = 1.0, jax.random.fold_in(rng, 6)
    for axis_at, shards_of in cuts:
        draws = jnp.exp(jax.random.uniform(jax.random.fold_in(own, axis_at), (shards_of,), jnp.float32, smallest / len(cuts), top_value / len(cuts)))
        gain = gain * jnp.repeat(draws, extent[axis_at] // shards_of).reshape([-1 if axis == axis_at else 1 for axis in range(len(extent))])
    return gain


def gaussian(rng, extent, deviation, most, cuts=(), dtype=jnp.bfloat16):
    values = jax.random.normal(rng, extent, jnp.float32) * deviation
    if len(cuts) > 0:
        values = shard_levels(rng, extent, cuts, -0.22, 0.18) * values
    return jnp.clip(values, min=-most, max=most).astype(dtype)


def setup_inputs(seed: int = 0) -> dict:
    keys = jax.random.split(jax.random.key(seed), 11)
    queries = gaussian(keys[0], (DOCS, LENGTH, WIDTH), 0.04, 0.23925781, ((0, 2), (1, 64), (2, 4)))
    key_rows = gaussian(keys[1], (DOCS, LENGTH, WIDTH), 0.04, 0.23925781, ((0, 2), (1, 64), (2, 4)))
    values = gaussian(keys[2], (DOCS, LENGTH, WIDTH), 1.0, 6.0, ((0, 2), (1, 64), (2, 4)))
    out_grad = gaussian(keys[3], (DOCS, LENGTH, WIDTH), 1.0, 6.0, ((0, 2), (1, 64), (2, 4)))
    decay_rate = draw_decay_rate(jax.random.fold_in(keys[10], 71), 0)
    rotation = draw_rotation(jax.random.fold_in(keys[10], 71), 0)
    refusal = draw_refusal(jax.random.fold_in(keys[10], 71), 0)
    proj_weight = gaussian(keys[7], (RANK, WIDTH), WIDTH ** -0.5, 0.09375, ((1, 4),), jnp.float32)
    proj_bias = gaussian(keys[8], (RANK,), 1.0, 4.0, (), jnp.float32)
    positions = draw_positions(jax.random.fold_in(keys[10], 71), 0)
    return {"queries": queries, "key_rows": key_rows, "values": values, "out_grad": out_grad, "decay_rate": decay_rate, "rotation": rotation, "refusal": refusal, "proj_weight": proj_weight, "proj_bias": proj_bias, "positions": positions}


highest = lax.Precision.HIGHEST


def decay_table(log_decay, count):
    offsets = jnp.arange(count)
    between = offsets[:, None] - offsets[None, :]
    powers = jnp.exp(jnp.maximum(between, 0).astype(jnp.float32)[None] * log_decay[:, None, None])
    return jnp.where(between[None] >= 0, powers, 0.0)


def gram_inverse(gram):
    determinant = gram[0, 0] * gram[1, 1] - gram[0, 1] * gram[1, 0]
    adjugate = jnp.stack([jnp.stack([gram[1, 1], -gram[0, 1]]), jnp.stack([-gram[1, 0], gram[0, 0]])])
    return adjugate / determinant


def reference(queries, key_rows, values, out_grad, decay_rate, rotation, refusal, proj_weight, proj_bias, positions):
    gram = jnp.dot(refusal.T, refusal, precision=highest)
    coupling = jnp.dot(rotation, refusal, precision=highest)
    inverse = gram_inverse(gram)
    rotated = rotation - jnp.dot(jnp.dot(coupling, inverse, precision=highest), refusal.T, precision=highest)
    log_decay = jnp.log1p(-decay_rate)
    table = decay_table(log_decay, GROUP)
    offsets = jnp.arange(GROUP).astype(jnp.float32)
    enter = jnp.exp((offsets + 1.0)[:, None] * log_decay[None, :])
    leave = jnp.exp((GROUP - offsets)[:, None] * log_decay[None, :])
    start_weight = jnp.exp(offsets[:, None] * log_decay[None, :])
    end_weight = jnp.exp((GROUP - 1.0 - offsets)[:, None] * log_decay[None, :])
    keep = jnp.exp(GROUP * log_decay)
    blocks = LENGTH // GROUP
    attended_all, grad_q_all, grad_k_all, grad_v_all = [], [], [], []
    grad_weight = jnp.zeros((RANK, WIDTH), jnp.float32)
    grad_bias = jnp.zeros((RANK,), jnp.float32)
    grad_rotated = jnp.zeros((RANK, WIDTH), jnp.float32)
    for document in range(DOCS):
        places = positions[document]
        picked = values[document][places].astype(jnp.float32)
        code = jnp.dot(picked, proj_weight.T, precision=highest) + proj_bias - jnp.dot(picked, rotated.T, precision=highest)
        shift_rows = jnp.dot(code, rotated, precision=highest)
        moved = values[document].at[places].set((picked + shift_rows).astype(jnp.bfloat16))
        query_blocks = queries[document].reshape(blocks, GROUP, HEADS, HDIM)
        key_blocks = key_rows[document].reshape(blocks, GROUP, HEADS, HDIM)
        moved_blocks = moved.reshape(blocks, GROUP, HEADS, HDIM)
        grad_blocks = out_grad[document].reshape(blocks, GROUP, HEADS, HDIM)

        def forward_block(state, block):
            query_b, key_b, moved_b = block
            scores = jnp.einsum('thd,shd->hts', query_b.astype(jnp.float32), key_b.astype(jnp.float32))
            mixing = (scores * table).astype(jnp.bfloat16)
            inner = jnp.einsum('hts,she->the', mixing.astype(jnp.float32), moved_b.astype(jnp.float32))
            outer = enter[:, :, None] * jnp.einsum('thd,hde->the', query_b.astype(jnp.float32), state, precision=highest)
            local = jnp.einsum('shd,she->hde', key_b.astype(jnp.float32) * end_weight[:, :, None], moved_b.astype(jnp.float32), precision=highest)
            return keep[:, None, None] * state + local, ((inner + outer).astype(jnp.bfloat16), state)

        start_state = jnp.zeros((HEADS, HDIM, HDIM), jnp.float32)
        _, (attended_blocks, entering) = lax.scan(forward_block, start_state, (query_blocks, key_blocks, moved_blocks))

        def backward_block(later, block):
            query_b, key_b, moved_b, grad_b, state = block
            scores = jnp.einsum('thd,shd->hts', query_b.astype(jnp.float32), key_b.astype(jnp.float32))
            mixing = (scores * table).astype(jnp.bfloat16)
            grad_scores = jnp.einsum('the,she->hts', grad_b.astype(jnp.float32), moved_b.astype(jnp.float32))
            grad_mixing = (grad_scores * table).astype(jnp.bfloat16)
            grad_q = jnp.einsum('hts,shd->thd', grad_mixing.astype(jnp.float32), key_b.astype(jnp.float32))
            grad_q = grad_q + enter[:, :, None] * jnp.einsum('the,hde->thd', grad_b.astype(jnp.float32), state, precision=highest)
            grad_k = jnp.einsum('hts,thd->shd', grad_mixing.astype(jnp.float32), query_b.astype(jnp.float32))
            grad_k = grad_k + leave[:, :, None] * jnp.einsum('she,hde->shd', moved_b.astype(jnp.float32), later, precision=highest)
            grad_m = jnp.einsum('hts,the->she', mixing.astype(jnp.float32), grad_b.astype(jnp.float32))
            grad_m = grad_m + leave[:, :, None] * jnp.einsum('shd,hde->she', key_b.astype(jnp.float32), later, precision=highest)
            local = jnp.einsum('thd,the->hde', query_b.astype(jnp.float32) * start_weight[:, :, None], grad_b.astype(jnp.float32), precision=highest)
            return keep[:, None, None] * later + local, (grad_q.astype(jnp.bfloat16), grad_k.astype(jnp.bfloat16), grad_m)

        _, (grad_q_blocks, grad_k_blocks, grad_m_blocks) = lax.scan(backward_block, start_state, (query_blocks, key_blocks, moved_blocks, grad_blocks, entering), reverse=True)
        grad_moved = grad_m_blocks.reshape(LENGTH, WIDTH)
        picked_grad = grad_moved[places]
        code_grad = jnp.dot(picked_grad, rotated.T, precision=highest)
        grad_weight = grad_weight + jnp.dot(code_grad.T, picked, precision=highest)
        grad_bias = grad_bias + jnp.sum(code_grad, axis=0)
        grad_rotated = grad_rotated + jnp.dot(code.T, picked_grad, precision=highest) - jnp.dot(code_grad.T, picked, precision=highest)
        grad_value = grad_moved.at[places].add(jnp.dot(code_grad, proj_weight - rotated, precision=highest))
        attended_all.append(attended_blocks.reshape(LENGTH, WIDTH))
        grad_q_all.append(grad_q_blocks.reshape(LENGTH, WIDTH))
        grad_k_all.append(grad_k_blocks.reshape(LENGTH, WIDTH))
        grad_v_all.append(grad_value.astype(jnp.bfloat16))
    along = jnp.dot(grad_rotated, refusal, precision=highest)
    grad_rotation = grad_rotated - jnp.dot(jnp.dot(along, inverse, precision=highest), refusal.T, precision=highest)
    return (jnp.stack(attended_all), jnp.stack(grad_q_all), jnp.stack(grad_k_all), jnp.stack(grad_v_all), grad_rotation, grad_weight, grad_bias)
```

```python
import functools
import jax
import jax.numpy as jnp
from jax import lax
from jax.experimental import pallas as pl
from jax.experimental.pallas import tpu as pltpu
from jax.sharding import Mesh, PartitionSpec as P

highest = lax.Precision.HIGHEST
f32, bf16 = jnp.float32, jnp.bfloat16
BLOCK = 128
HEADS = 8
SIZE = 128
WIDE = HEADS * SIZE
NPOS = 16
NEAR = ("zl", "y")
SMEM = pl.BlockSpec(memory_space=pltpu.SMEM)
VMEM = pl.BlockSpec(memory_space=pltpu.VMEM)


def nn(a, b):
    return lax.dot_general(a, b, (((1,), (0,)), ((), ())), preferred_element_type=f32)


def nt(a, b):
    return lax.dot_general(a, b, (((1,), (1,)), ((), ())), preferred_element_type=f32)


def tn(a, b):
    return lax.dot_general(a, b, (((0,), (0,)), ((), ())), preferred_element_type=f32)


def full_nt(a, b):
    return lax.dot_general(
        a, b, (((1,), (1,)), ((), ())), preferred_element_type=f32, precision=highest
    )


def full_tn(a, b):
    return lax.dot_general(
        a, b, (((0,), (0,)), ((), ())), preferred_element_type=f32, precision=highest
    )


def split(x):
    high = x.astype(bf16)
    return high, (x - high.astype(f32)).astype(bf16)


def log_keep(rate):
    total = jnp.float32(1.0 / 8.0)
    for n in range(7, 0, -1):
        total = total * rate + jnp.float32(1.0 / n)
    return -rate * total


def powers(rate, exponents):
    return jnp.exp(exponents * log_keep(rate))


def rows_iota(shape=(BLOCK, SIZE)):
    return lax.broadcasted_iota(jnp.int32, shape, 0)


def cols_iota(shape=(BLOCK, SIZE)):
    return lax.broadcasted_iota(jnp.int32, shape, 1)


def selector(positions, start):
    row = rows_iota((NPOS, BLOCK))
    place = cols_iota((NPOS, BLOCK)) + start
    wanted = jnp.full((NPOS, BLOCK), -1, jnp.int32)
    for j in range(NPOS):
        wanted = jnp.where(row == j, positions[0, j], wanted)
    return (wanted == place).astype(f32)


def head_cols(h):
    return slice(h * SIZE, (h + 1) * SIZE)


def decayed_state(weighted, other):
    high, low = split(weighted)
    return tn(other, high) + tn(other, low)


def query_state(meta, rate, positions, q, grad, v, rot, ref, proj, state, small, picked):
    offset = rows_iota().astype(f32)
    for h in range(HEADS):
        c = head_cols(h)
        weighted = q[:, c].astype(f32) * powers(rate[h], offset)
        out = decayed_state(weighted, grad[:, c])
        state[2 * h] = out[:64]
        state[2 * h + 1] = out[64:]
    select = selector(positions, meta[0])
    chosen = nn(select.astype(bf16), v[...])
    picked[...] = chosen
    left = jnp.concatenate([chosen, ref[...], rot[...], jnp.zeros((2, WIDE), f32)], axis=0)
    right = jnp.concatenate(
        [proj[...] - rot[...], ref[...], rot[...], jnp.zeros((6, WIDE), f32)], axis=0
    )
    small[...] = jnp.zeros((24, 128), f32)
    small[:, 0:16] = full_nt(left, right)


def inverse_of(small):
    g00, g01 = small[16:17, 4:5], small[16:17, 5:6]
    g10, g11 = small[17:18, 4:5], small[17:18, 5:6]
    det = g00 * g11 - g01 * g10
    return g11 / det, -g01 / det, -g10 / det, g00 / det


def key_state(meta, rate, positions, small, v, k, rot, ref, bias, moved, state, basis, code):
    i00, i01, i10, i11 = inverse_of(small)
    c0, c1 = small[18:22, 4:5], small[18:22, 5:6]
    rotated = (
        rot[...]
        - (c0 * i00 + c1 * i10) * ref[0:1, :]
        - (c0 * i01 + c1 * i11) * ref[1:2, :]
    )
    basis[...] = jnp.concatenate([rotated, ref[...], jnp.zeros((2, WIDE), f32)], axis=0)
    turned = pltpu.roll(small[16:24, :], 122, 1)
    t0, t1 = turned[0:1], turned[1:2]
    full = (
        small[0:16, :]
        + bias[...]
        + small[0:16, 4:5] * (t0 * i00 + t1 * i10)
        + small[0:16, 5:6] * (t0 * i01 + t1 * i11)
    )
    full = jnp.where(cols_iota((NPOS, 128)) < 4, full, 0.0)
    code[...] = full
    shift = jnp.zeros((NPOS, WIDE), f32)
    for r in range(4):
        shift = shift + full[:, r : r + 1] * rotated[r : r + 1, :]
    select = selector(positions, meta[0])
    offset = rows_iota().astype(f32)
    for h in range(HEADS):
        c = head_cols(h)
        new = (v[:, c].astype(f32) + full_tn(select, shift[:, c])).astype(bf16)
        moved[:, c] = new
        weighted = k[:, c].astype(f32) * powers(rate[h], BLOCK - 1.0 - offset)
        out = decayed_state(weighted, new)
        state[2 * h] = out[:64]
        state[2 * h + 1] = out[64:]


def inside(rate, q, k, moved, grad, attended, grad_q, grad_k, grad_m):
    between = rows_iota() - cols_iota()
    lower = between >= 0
    distance = jnp.maximum(between, 0).astype(f32)
    for h in range(HEADS):
        c = head_cols(h)
        table = jnp.where(lower, powers(rate[h], distance), 0.0)
        qh, kh, mh, gh = q[:, c], k[:, c], moved[:, c], grad[:, c]
        mixing = (nt(qh, kh) * table).astype(bf16)
        grad_mixing = (nt(gh, mh) * table).astype(bf16)
        attended[:, c] = nn(mixing, mh)
        grad_q[:, c] = nn(grad_mixing, kh)
        grad_k[:, c] = tn(grad_mixing, qh)
        grad_m[:, c] = tn(mixing, gh)


def group_totals(meta, rate, later, earlier, out):
    far, near = meta[1], meta[2]
    keep = powers(rate[near // 2], jnp.full((64, 128), float(BLOCK), f32))
    forward = earlier[0]
    backward = later[15]
    for b in range(1, 16):
        forward = forward * keep + earlier[b]
        backward = backward * keep + later[15 - b]
    for z in range(4):
        out[z] = jnp.where(far < z, forward, backward)


def carried(meta, rate, later, earlier, others, leaving, entering):
    far, near = meta[1], meta[2]
    exponent = jnp.full((64, 128), float(BLOCK), f32)
    keep = powers(rate[near // 2], exponent)
    keep_group = powers(rate[near // 2], exponent * 16.0)
    forward = jnp.zeros((64, 128), f32)
    backward = jnp.zeros((64, 128), f32)
    for z in range(3):
        forward = jnp.where(far > z, forward * keep_group + others[z], forward)
        backward = jnp.where(far < 3 - z, backward * keep_group + others[3 - z], backward)
    for b in range(16):
        entering[b] = forward
        forward = forward * keep + earlier[b]
        leaving[15 - b] = backward
        backward = backward * keep + later[15 - b]


def backward_rest(
    meta, rate, positions, k, moved, state, grad_k_in, grad_m_in, basis, grad_k, grad_m, picked, small
):
    offset = rows_iota().astype(f32)
    select = selector(positions, meta[0])
    for h in range(HEADS):
        c = head_cols(h)
        leave = powers(rate[h], BLOCK - offset)
        high, low = split(jnp.concatenate([state[2 * h], state[2 * h + 1]], axis=0))
        mh, kh = moved[:, c], k[:, c]
        grad_k[:, c] = (grad_k_in[:, c] + leave * (nn(mh, high) + nn(mh, low))).astype(bf16)
        out = grad_m_in[:, c] + leave * (nt(kh, high) + nt(kh, low))
        grad_m[:, c] = out
        picked[:, c] = lax.dot_general(
            select, out, (((1,), (0,)), ((), ())), preferred_element_type=f32, precision=highest
        )
    small[...] = jnp.zeros((NPOS, 128), f32)
    small[:, 0:8] = full_nt(picked[...], basis[...])


def forward_rest(rate, q, grad, state, attended_in, grad_q_in, attended, grad_q):
    offset = rows_iota().astype(f32)
    for h in range(HEADS):
        c = head_cols(h)
        enter = powers(rate[h], offset + 1.0)
        high, low = split(jnp.concatenate([state[2 * h], state[2 * h + 1]], axis=0))
        qh, gh = q[:, c], grad[:, c]
        attended[:, c] = (attended_in[:, c] + enter * (nt(qh, high) + nt(qh, low))).astype(bf16)
        grad_q[:, c] = (grad_q_in[:, c] + enter * (nn(gh, high) + nn(gh, low))).astype(bf16)


def value_rest(
    meta, positions, small_grad, small, code, picked, picked_grad, grad_m, proj, basis, grad_v, parts
):
    code_grad = jnp.where(cols_iota((NPOS, 128)) < 4, small_grad[...], 0.0)
    lift = proj[...] - basis[0:4, :]
    fix = jnp.zeros((NPOS, WIDE), f32)
    for r in range(4):
        fix = fix + code_grad[:, r : r + 1] * lift[r : r + 1, :]
    select = selector(positions, meta[0])
    for h in range(HEADS):
        c = head_cols(h)
        grad_v[:, c] = (grad_m[:, c] + full_tn(select, fix[:, c])).astype(bf16)
    weight = full_tn(code_grad, picked[...])
    turn = full_tn(code[...], picked_grad[...])
    along = full_tn(code[...], small_grad[...]) - full_tn(code_grad, small[0:16, :])
    bias = full_tn(code_grad, jnp.ones((NPOS, 128), f32))
    lane = cols_iota((4, 128))
    extra = jnp.where(lane < 4, bias[0:4], along[0:4])
    for i in range(8):
        c = head_cols(i)
        parts[i] = jnp.concatenate([weight[0:4, c], extra], axis=0)
        parts[8 + i] = jnp.concatenate([turn[0:4, c], extra], axis=0)


def finish(small, ref, parts, grad_rotation, grad_weight, grad_bias):
    i00, i01, i10, i11 = inverse_of(small)
    extra = parts[0]
    a0, a1 = extra[4:8, 4:5], extra[4:8, 5:6]
    b0 = a0 * i00 + a1 * i10
    b1 = a0 * i01 + a1 * i11
    for i in range(8):
        c = head_cols(i)
        weight = parts[i][0:4]
        grad_weight[:, c] = weight
        grad_rotation[:, c] = (
            parts[8 + i][0:4] - weight - b0 * ref[0:1, c] - b1 * ref[1:2, c]
        )
    grad_bias[...] = extra[4:8, :]


def call(kernel, specs, outs, flops=1e8, bytes_accessed=2e6):
    return pl.pallas_call(
        kernel,
        in_specs=[SMEM if s == "s" else VMEM for s in specs],
        out_specs=[VMEM] * len(outs),
        out_shape=[jax.ShapeDtypeStruct(s, d) for s, d in outs],
        compiler_params=pltpu.CompilerParams(vmem_limit_bytes=40 * 1024 * 1024),
        cost_estimate=pl.CostEstimate(
            flops=int(flops), bytes_accessed=int(bytes_accessed), transcendentals=0
        ),
    )


def swap(x, axes):
    return lax.all_to_all(x, axes, 0, 0, tiled=False)


def shards(queries, key_rows, values, out_grad, rate, rotation, refusal, proj_weight, proj_bias, positions):
    q, k, v, grad = queries[0], key_rows[0], values[0], out_grad[0]
    ref = refusal.T
    far, near = lax.axis_index("zh"), lax.axis_index(NEAR)
    meta = jnp.stack([(far * 16 + near) * BLOCK, far, near]).astype(jnp.int32)
    bias = jnp.pad(proj_bias, (0, 124))[None, :]
    rows = (BLOCK, WIDE)
    pieces = (16, 64, 128)

    grad_state, small, picked = call(
        query_state, "sssvvvvvv", [(pieces, f32), ((24, 128), f32), ((NPOS, WIDE), f32)]
    )(meta, rate, positions, q, grad, v, rotation, ref, proj_weight)
    grad_pieces = swap(grad_state, NEAR)
    small = lax.psum(small, "head")
    moved, state, basis, code = call(
        key_state,
        "sssvvvvvv",
        [(rows, bf16), (pieces, f32), ((8, WIDE), f32), ((NPOS, 128), f32)],
    )(meta, rate, positions, small, v, k, rotation, ref, bias)
    pieces_in = swap(state, NEAR)
    attended_in, grad_q_in, grad_k_in, grad_m_in = call(inside, "svvvv", [(rows, f32)] * 4)(
        rate, q, k, moved, grad
    )
    (totals,) = call(group_totals, "ssvv", [((4, 64, 128), f32)])(meta, rate, grad_pieces, pieces_in)
    others = swap(totals, "zh")
    leaving, entering = call(carried, "ssvvv", [(pieces, f32)] * 2)(
        meta, rate, grad_pieces, pieces_in, others
    )
    leaving = swap(leaving, NEAR)
    grad_k, grad_m, picked_grad, small_grad = call(
        backward_rest,
        "sssvvvvvv",
        [(rows, bf16), (rows, f32), ((NPOS, WIDE), f32), ((NPOS, 128), f32)],
    )(meta, rate, positions, k, moved, leaving, grad_k_in, grad_m_in, basis)
    entering = swap(entering, NEAR)
    small_grad = lax.psum(small_grad, "head")
    grad_v, parts = call(value_rest, "ssvvvvvvvv", [(rows, bf16), ((16, 8, 128), f32)])(
        meta, positions, small_grad, small, code, picked, picked_grad, grad_m, proj_weight, basis
    )
    part = jnp.sum(swap(parts, NEAR), axis=0)
    attended, grad_q = call(forward_rest, "svvvvv", [(rows, bf16)] * 2)(
        rate, q, grad, entering, attended_in, grad_q_in
    )
    part = lax.psum(lax.psum(part, "zh"), "dp")
    parts = swap(jnp.broadcast_to(part[None], (16, 8, 128)), NEAR)
    grad_rotation, grad_weight, grad_bias = call(
        finish, "vvv", [((4, WIDE), f32), ((4, WIDE), f32), ((4, 128), f32)]
    )(small, ref, parts)
    return (
        attended[None],
        grad_q[None],
        grad_k[None],
        grad_v[None],
        grad_rotation,
        grad_weight,
        grad_bias[:, 0],
    )


def solution(mesh):
    own = Mesh(mesh.devices.reshape(4, 4, 4, 4, 2), ("zh", "zl", "y", "head", "dp"))
    seq = ("zh", "zl", "y")
    stream = P("dp", seq, "head")
    return jax.shard_map(
        shards,
        mesh=own,
        in_specs=(
            stream,
            stream,
            stream,
            stream,
            P("head"),
            P(None, "head"),
            P("head", None),
            P(None, "head"),
            P(),
            P("dp", None),
        ),
        out_specs=(stream, stream, stream, stream, P(None, "head"), P(None, "head"), P()),
        check_vma=False,
    )
```

```python
import functools
import jax
import jax.numpy as jnp
from jax import lax
from jax.experimental import pallas as pl
from jax.experimental.pallas import tpu as pltpu
from jax.sharding import Mesh, PartitionSpec as P

highest = lax.Precision.HIGHEST
f32, bf16 = jnp.float32, jnp.bfloat16
BLOCK = 128
HEADS = 8
SIZE = 128
WIDE = HEADS * SIZE
NPOS = 16
NEAR = ("zl", "y")
SMEM = pl.BlockSpec(memory_space=pltpu.SMEM)
VMEM = pl.BlockSpec(memory_space=pltpu.VMEM)


def nn(a, b):
    return lax.dot_general(a, b, (((1,), (0,)), ((), ())), preferred_element_type=f32)


def nt(a, b):
    return lax.dot_general(a, b, (((1,), (1,)), ((), ())), preferred_element_type=f32)


def tn(a, b):
    return lax.dot_general(a, b, (((0,), (0,)), ((), ())), preferred_element_type=f32)


def full_nt(a, b):
    return lax.dot_general(
        a, b, (((1,), (1,)), ((), ())), preferred_element_type=f32, precision=highest
    )


def full_tn(a, b):
    return lax.dot_general(
        a, b, (((0,), (0,)), ((), ())), preferred_element_type=f32, precision=highest
    )


def split(x):
    high = x.astype(bf16)
    return high, (x - high.astype(f32)).astype(bf16)


def log_keep(rate):
    total = jnp.float32(1.0 / 8.0)
    for n in range(7, 0, -1):
        total = total * rate + jnp.float32(1.0 / n)
    return -rate * total


def powers(rate, exponents):
    return jnp.exp(exponents * log_keep(rate))


def rows_iota(shape=(BLOCK, SIZE)):
    return lax.broadcasted_iota(jnp.int32, shape, 0)


def cols_iota(shape=(BLOCK, SIZE)):
    return lax.broadcasted_iota(jnp.int32, shape, 1)


def local_places(positions, start):
    row = rows_iota((NPOS, BLOCK))
    wanted = jnp.full((NPOS, BLOCK), -1, jnp.int32)
    for j in range(NPOS):
        wanted = jnp.where(row == j, positions[0, j], wanted)
    return wanted - start


def selector(positions, start):
    return (local_places(positions, start) == cols_iota((NPOS, BLOCK))).astype(f32)


def head_cols(h):
    return slice(h * SIZE, (h + 1) * SIZE)


def decayed_state(weighted, other):
    high, low = split(weighted)
    return tn(other, high) + tn(other, low)


def halves(left, right, odd):
    lane = cols_iota(left.shape)
    if odd:
        return jnp.where(lane < 64, pltpu.roll(left, 64, 1), right)
    return jnp.where(lane < 64, left, pltpu.roll(right, 64, 1))


def query_state(meta, rate, positions, q, k, grad, v, rot, ref, proj, out, small):
    offset = rows_iota().astype(f32)
    places = local_places(positions, meta[0])
    lane = cols_iota((NPOS, BLOCK))
    select = (places == lane).astype(bf16)
    after = lane - places
    reached = after >= 0
    distance = jnp.maximum(after, 0).astype(f32)
    leave = jnp.clip(BLOCK - places, 0, BLOCK).astype(f32)
    chosen = nn(select, v[...])
    for h in range(HEADS):
        c = head_cols(h)
        weighted = q[:, c].astype(f32) * powers(rate[h], offset)
        state = decayed_state(weighted, grad[:, c])
        key = nn(select, k[:, c])
        table = jnp.where(reached, powers(rate[h], distance), 0.0)
        mixing = (nt(key.astype(bf16), q[:, c]) * table).astype(bf16)
        local = nn(mixing, grad[:, c])
        key = key * powers(rate[h], leave)
        for odd in range(2):
            i = 2 * h + odd
            out[i, 0:64] = state[64 * odd : 64 * odd + 64]
            out[i, 64:80] = key
            out[i, 80:96] = halves(local, chosen[:, c], odd)
    left = jnp.concatenate([chosen, ref[...], rot[...], jnp.zeros((2, WIDE), f32)], axis=0)
    right = jnp.concatenate(
        [proj[...] - rot[...], ref[...], rot[...], jnp.zeros((6, WIDE), f32)], axis=0
    )
    small[...] = jnp.zeros((24, 128), f32)
    small[:, 0:16] = full_nt(left, right)


def inverse_of(small):
    g00, g01 = small[16:17, 4:5], small[16:17, 5:6]
    g10, g11 = small[17:18, 4:5], small[17:18, 5:6]
    det = g00 * g11 - g01 * g10
    return g11 / det, -g01 / det, -g10 / det, g00 / det


def key_state(meta, rate, positions, small, v, k, rot, ref, proj, bias, moved, state, basis):
    i00, i01, i10, i11 = inverse_of(small)
    c0, c1 = small[18:22, 4:5], small[18:22, 5:6]
    rotated = (
        rot[...]
        - (c0 * i00 + c1 * i10) * ref[0:1, :]
        - (c0 * i01 + c1 * i11) * ref[1:2, :]
    )
    lift = proj[...] - rotated
    rows = jnp.concatenate(
        [rotated, ref[...], lift, ref[...], jnp.zeros((4, WIDE), f32)], axis=0
    )
    turned = pltpu.roll(small[16:24, :], 122, 1)
    t0, t1 = turned[0:1], turned[1:2]
    full = (
        small[0:16, :]
        + bias[...]
        + small[0:16, 4:5] * (t0 * i00 + t1 * i10)
        + small[0:16, 5:6] * (t0 * i01 + t1 * i11)
    )
    full = jnp.where(cols_iota((NPOS, 128)) < 4, full, 0.0)
    shift = jnp.zeros((NPOS, WIDE), f32)
    for r in range(4):
        shift = shift + full[:, r : r + 1] * rotated[r : r + 1, :]
    select = selector(positions, meta[0])
    offset = rows_iota().astype(f32)
    for h in range(HEADS):
        c = head_cols(h)
        basis[h] = rows[:, c]
        new = (v[:, c].astype(f32) + full_tn(select, shift[:, c])).astype(bf16)
        moved[:, c] = new
        weighted = k[:, c].astype(f32) * powers(rate[h], BLOCK - 1.0 - offset)
        out = decayed_state(weighted, new)
        state[2 * h] = out[:64]
        state[2 * h + 1] = out[64:]


def inside(rate, q, k, moved, grad, attended, grad_q, mixings, grad_mixings):
    between = rows_iota() - cols_iota()
    lower = between >= 0
    distance = jnp.maximum(between, 0).astype(f32)
    for h in range(HEADS):
        c = head_cols(h)
        table = jnp.where(lower, powers(rate[h], distance), 0.0)
        qh, kh, mh, gh = q[:, c], k[:, c], moved[:, c], grad[:, c]
        mixing = (nt(qh, kh) * table).astype(bf16)
        grad_mixing = (nt(gh, mh) * table).astype(bf16)
        mixings[h] = mixing
        grad_mixings[h] = grad_mixing
        attended[:, c] = nn(mixing, mh)
        grad_q[:, c] = nn(grad_mixing, kh)


def dot3(a, b):
    ah, al = split(a)
    bh, bl = split(b)
    return nt(ah, bh) + (nt(al, bh) + nt(ah, bl))


def backward_totals(meta, rate, later, out, gathered):
    keep = powers(rate[meta[2] // 2], jnp.full((64, 128), float(BLOCK), f32))
    keep_key = keep[0:NPOS]
    state = later[15, 0:64]
    key = later[0, 64:80]
    rows = later[15, 80:96]
    gathered[...] = jnp.zeros((NPOS, 128), f32)
    for b in range(14, -1, -1):
        gathered[:, 0:64] += dot3(later[b, 64:80], state)
        rows = rows + later[b, 80:96]
        state = state * keep + later[b, 0:64]
    for b in range(1, 16):
        key = key * keep_key + later[b, 64:80]
    out[0:64] = state
    out[64:80] = key
    out[80:96] = rows + gathered[...]


def backward_carried(
    meta, rate, later, own, one, two, three, basis, out, pairs, groups, gathered
):
    far, near = meta[1], meta[2]
    exponent = jnp.full((64, 128), float(BLOCK), f32)
    keep = powers(rate[near // 2], exponent)
    keep_group = powers(rate[near // 2], exponent * 16.0)
    for d, part in enumerate((own, one, two, three)):
        groups[(far + 4 - d) % 4] = part[...]
    rows = groups[3, 80:96]
    gathered[...] = jnp.zeros((NPOS, 128), f32)
    carry = jnp.zeros((64, 128), f32)
    state = carry
    for z in (2, 1, 0):
        carry = carry * keep_group + groups[z + 1, 0:64]
        gathered[:, 0:64] += dot3(groups[z, 64:80], carry)
        rows = rows + groups[z, 80:96]
        state = jnp.where(far == z, carry, state)
    rows = rows + gathered[...]
    both = basis[near // 2]
    turned = pltpu.roll(both, 64, 1)
    odd = near % 2 == 1
    lane, row = cols_iota((16, 128)), rows_iota((16, 128))
    for_grad = jnp.where(odd, turned, both)
    for_value = jnp.where(odd, both, turned)
    right = jnp.where(
        row < 6,
        jnp.where(lane < 64, for_grad, 0.0),
        jnp.where(lane < 64, 0.0, for_value),
    )
    gathered[...] = jnp.zeros((NPOS, 128), f32)
    gathered[:, 0:16] = full_nt(rows, right)
    for b in range(15, -1, -1):
        out[b, 0:64] = state
        out[b, 64:80] = gathered[...]
        state = state * keep + later[b, 0:64]
    pairs[...] = rows


def forward_totals(meta, rate, earlier, out):
    keep = powers(rate[meta[2] // 2], jnp.full((64, 128), float(BLOCK), f32))
    state = earlier[0]
    for b in range(1, 16):
        state = state * keep + earlier[b]
    out[...] = state


def forward_carried(meta, rate, earlier, one, two, three, parts, out):
    exponent = jnp.full((64, 128), float(BLOCK), f32)
    keep = powers(rate[meta[2] // 2], exponent)
    keep_group = powers(rate[meta[2] // 2], exponent * 16.0)
    state = (three[...] * keep_group + two[...]) * keep_group + one[...]
    for b in range(16):
        out[b, 0:64] = state
        out[b, 64:72] = parts[...]
        state = state * keep + earlier[b]


def sum_slices(x, out):
    total = x[0, 64:80]
    for i in range(1, 16):
        total = total + x[i, 64:80]
    out[...] = total


def products(head_sums, bias, pairs, parts):
    lane = cols_iota((NPOS, 128))
    sums = head_sums[...]
    code_grad = jnp.where(lane < 4, sums, 0.0)
    code = jnp.where(lane < 4, pltpu.roll(sums, 122, 1) + bias[...], 0.0)
    values_along = pltpu.roll(sums, 122, 1)
    turn = full_tn(code, pairs[...])[0:4]
    weight = full_tn(code_grad, pairs[...])[0:4]
    along = (full_tn(code, sums) - full_tn(code_grad, values_along))[0:4]
    total = full_tn(code_grad, jnp.ones((NPOS, 128), f32))[0:4]
    lane = cols_iota((4, 128))
    parts[...] = jnp.concatenate(
        [jnp.where(lane < 64, turn, weight), jnp.where(lane < 4, total, along)], axis=0
    )


def backward_rest(
    meta, rate, positions, q, k, moved, grad, state, mixings, grad_mixings, basis, head_sums,
    grad_k, grad_v,
):
    offset = rows_iota().astype(f32)
    select = selector(positions, meta[0])
    code_grad = head_sums[...]
    for h in range(HEADS):
        c = head_cols(h)
        leave = powers(rate[h], BLOCK - offset)
        high, low = split(jnp.concatenate([state[2 * h, 0:64], state[2 * h + 1, 0:64]], axis=0))
        qh, mh, kh, gh = q[:, c], moved[:, c], k[:, c], grad[:, c]
        inner = tn(grad_mixings[h], qh)
        grad_k[:, c] = (inner + leave * (nn(mh, high) + nn(mh, low))).astype(bf16)
        inner = tn(mixings[h], gh)
        lift = basis[h][6:10]
        fix = jnp.zeros((NPOS, SIZE), f32)
        for r in range(4):
            fix = fix + code_grad[:, r : r + 1] * lift[r : r + 1]
        out = inner + leave * (nt(kh, high) + nt(kh, low))
        grad_v[:, c] = (out + full_tn(select, fix)).astype(bf16)


def forward_rest(
    rate, q, grad, state, attended_in, grad_q_in, small, ref, parts,
    attended, grad_q, grad_rotation, grad_weight, grad_bias,
):
    offset = rows_iota().astype(f32)
    i00, i01, i10, i11 = inverse_of(small)
    a0, a1 = parts[4:8, 4:5], parts[4:8, 5:6]
    b0 = a0 * i00 + a1 * i10
    b1 = a0 * i01 + a1 * i11
    lane = cols_iota((8, 128))
    for h in range(HEADS):
        c = head_cols(h)
        enter = powers(rate[h], offset + 1.0)
        high, low = split(jnp.concatenate([state[2 * h, 0:64], state[2 * h + 1, 0:64]], axis=0))
        qh, gh = q[:, c], grad[:, c]
        attended[:, c] = (attended_in[:, c] + enter * (nt(qh, high) + nt(qh, low))).astype(bf16)
        grad_q[:, c] = (grad_q_in[:, c] + enter * (nn(gh, high) + nn(gh, low))).astype(bf16)
        even, odd = state[2 * h, 64:72], state[2 * h + 1, 64:72]
        turn = jnp.where(lane < 64, even, pltpu.roll(odd, 64, 1))[0:4]
        weight = jnp.where(lane < 64, pltpu.roll(even, 64, 1), odd)[0:4]
        grad_weight[:, c] = weight
        grad_rotation[:, c] = turn - weight - b0 * ref[0:1, c] - b1 * ref[1:2, c]
    grad_bias[...] = parts[4:8, :]


def call(kernel, specs, outs, scratch=(), flops=1e8, bytes_accessed=2e6):
    return pl.pallas_call(
        kernel,
        in_specs=[SMEM if s == "s" else VMEM for s in specs],
        out_specs=[VMEM] * len(outs),
        out_shape=[jax.ShapeDtypeStruct(s, d) for s, d in outs],
        scratch_shapes=[pltpu.VMEM(s, f32) for s in scratch],
        compiler_params=pltpu.CompilerParams(vmem_limit_bytes=40 * 1024 * 1024),
        cost_estimate=pl.CostEstimate(
            flops=int(flops), bytes_accessed=int(bytes_accessed), transcendentals=0
        ),
    )


def swap(x, axes):
    return lax.all_to_all(x, axes, 0, 0, tiled=False)


def ahead(x, d):
    return lax.ppermute(x, "zh", [(i, i + d) for i in range(4 - d)])


def round_by(x, d):
    return lax.ppermute(x, "zh", [(i, (i + d) % 4) for i in range(4)])


def shards(queries, key_rows, values, out_grad, rate, rotation, refusal, proj_weight, proj_bias, positions):
    q, k, v, grad = queries[0], key_rows[0], values[0], out_grad[0]
    ref = refusal.T
    far, near = lax.axis_index("zh"), lax.axis_index(NEAR)
    meta = jnp.stack([(far * 16 + near) * BLOCK, far, near]).astype(jnp.int32)
    bias = jnp.pad(proj_bias, (0, 124))[None, :]
    rows = (BLOCK, WIDE)
    tile = (NPOS, 128)
    square = (HEADS, BLOCK, BLOCK)

    grad_state, small = call(
        query_state, "sssvvvvvvv", [((16, 96, 128), f32), ((24, 128), f32)]
    )(meta, rate, positions, q, k, grad, v, rotation, ref, proj_weight)
    later = swap(grad_state, NEAR)
    small = lax.psum(small, "head")
    moved, state, basis = call(
        key_state,
        "sssvvvvvvv",
        [(rows, bf16), ((16, 64, 128), f32), ((HEADS, 16, 128), f32)],
    )(meta, rate, positions, small, v, k, rotation, ref, proj_weight, bias)
    (own,) = call(backward_totals, "ssv", [((96, 128), f32)], [tile])(meta, rate, later)
    around = [round_by(own, d) for d in (1, 2, 3)]
    state, own = lax.optimization_barrier((state, own))
    earlier = swap(state, NEAR)
    leaving, pairs = call(
        backward_carried,
        "ssvvvvvv",
        [((16, 80, 128), f32), (tile, f32)],
        [(4, 96, 128), tile],
    )(meta, rate, later, own, *around, basis)
    (total,) = call(forward_totals, "ssv", [((64, 128), f32)])(meta, rate, earlier)
    passed = [ahead(total, d) for d in (1, 2, 3)]
    leaving, total = lax.optimization_barrier((leaving, total))
    leaving = swap(leaving, NEAR)
    attended_in, grad_q_in, mixings, grad_mixings = call(
        inside, "svvvv", [(rows, f32)] * 2 + [(square, bf16)] * 2
    )(rate, q, k, moved, grad)
    (head_sums,) = call(sum_slices, "v", [(tile, f32)])(leaving)
    head_sums = lax.psum(head_sums, "head")
    (parts,) = call(products, "vvv", [((8, 128), f32)])(head_sums, bias, pairs)
    parts = lax.psum(parts, "dp")
    (entering,) = call(forward_carried, "ssvvvvv", [((16, 72, 128), f32)])(
        meta, rate, earlier, *passed, parts
    )
    entering = swap(entering, NEAR)
    grad_k, grad_v = call(backward_rest, "sssvvvvvvvvv", [(rows, bf16)] * 2)(
        meta, rate, positions, q, k, moved, grad, leaving, mixings, grad_mixings, basis, head_sums
    )
    attended, grad_q, grad_rotation, grad_weight, grad_bias = call(
        forward_rest,
        "svvvvvvvv",
        [(rows, bf16)] * 2 + [((4, WIDE), f32)] * 2 + [((4, 128), f32)],
    )(rate, q, grad, entering, attended_in, grad_q_in, small, ref, parts)
    return (
        attended[None],
        grad_q[None],
        grad_k[None],
        grad_v[None],
        grad_rotation,
        grad_weight,
        grad_bias[:, 0],
    )


def solution(mesh):
    own = Mesh(mesh.devices.reshape(4, 4, 4, 4, 2), ("zh", "zl", "y", "head", "dp"))
    seq = ("zh", "zl", "y")
    stream = P("dp", seq, "head")
    return jax.shard_map(
        shards,
        mesh=own,
        in_specs=(
            stream,
            stream,
            stream,
            stream,
            P("head"),
            P(None, "head"),
            P("head", None),
            P(None, "head"),
            P(),
            P("dp", None),
        ),
        out_specs=(stream, stream, stream, stream, P(None, "head"), P(None, "head"), P()),
        check_vma=False,
    )
```

```python
import functools
import jax
import jax.numpy as jnp
from jax import lax
from jax.experimental import pallas as pl
from jax.experimental.pallas import tpu as pltpu
from jax.sharding import Mesh, PartitionSpec as P

highest = lax.Precision.HIGHEST
f32, bf16 = jnp.float32, jnp.bfloat16
BLOCK = 128
HEADS = 8
SIZE = 128
WIDE = HEADS * SIZE
NPOS = 16
NEAR = ("zl", "y")
ANY = pl.BlockSpec(memory_space=pltpu.HBM)
SMEM = pl.BlockSpec(memory_space=pltpu.SMEM)
VMEM = pl.BlockSpec(memory_space=pltpu.VMEM)


def nn(a, b):
    return lax.dot_general(a, b, (((1,), (0,)), ((), ())), preferred_element_type=f32)


def nt(a, b):
    return lax.dot_general(a, b, (((1,), (1,)), ((), ())), preferred_element_type=f32)


def tn(a, b):
    return lax.dot_general(a, b, (((0,), (0,)), ((), ())), preferred_element_type=f32)


def full_nt(a, b):
    return lax.dot_general(
        a, b, (((1,), (1,)), ((), ())), preferred_element_type=f32, precision=highest
    )


def full_tn(a, b):
    return lax.dot_general(
        a, b, (((0,), (0,)), ((), ())), preferred_element_type=f32, precision=highest
    )


def split(x):
    high = x.astype(bf16)
    return high, (x - high.astype(f32)).astype(bf16)


def log_keep(rate):
    total = jnp.float32(1.0 / 8.0)
    for n in range(7, 0, -1):
        total = total * rate + jnp.float32(1.0 / n)
    return -rate * total


def powers(rate, exponents):
    return jnp.exp(exponents * log_keep(rate))


def rows_iota(shape=(BLOCK, SIZE)):
    return lax.broadcasted_iota(jnp.int32, shape, 0)


def cols_iota(shape=(BLOCK, SIZE)):
    return lax.broadcasted_iota(jnp.int32, shape, 1)


def far_place():
    return lax.axis_index("zh")


def near_place():
    return lax.axis_index("zl") * 4 + lax.axis_index("y")


def block_start():
    return (far_place() * 16 + near_place()) * BLOCK


def local_places(positions, start):
    row = rows_iota((NPOS, BLOCK))
    wanted = jnp.full((NPOS, BLOCK), -1, jnp.int32)
    for j in range(NPOS):
        wanted = jnp.where(row == j, positions[0, j], wanted)
    return wanted - start


def selector(positions, start):
    return (local_places(positions, start) == cols_iota((NPOS, BLOCK))).astype(f32)


def head_cols(h):
    return slice(h * SIZE, (h + 1) * SIZE)


def decayed_state(weighted, other):
    high, low = split(weighted)
    return tn(other, high) + tn(other, low)


def halves(left, right, odd):
    lane = cols_iota(left.shape)
    if odd:
        return jnp.where(lane < 64, pltpu.roll(left, 64, 1), right)
    return jnp.where(lane < 64, left, pltpu.roll(right, 64, 1))


def query_state(
    rate, positions, q_far, k_far, grad_far, v_far, rot, ref, proj, out_far, small,
    q, k, grad, v, out, chosen, arrived, sent,
):
    fetches = []
    for part in range(4):
        c = slice(part * 2 * SIZE, (part + 1) * 2 * SIZE)
        pairs = ((q_far, q), (grad_far, grad), (k_far, k), (v_far, v))
        for n, (src, dst) in enumerate(pairs):
            fetch = pltpu.make_async_copy(src.at[:, c], dst.at[:, c], arrived.at[part, n])
            fetch.start()
            fetches.append(fetch)
    sends = []
    offset = rows_iota().astype(f32)
    places = local_places(positions, block_start())
    lane = cols_iota((NPOS, BLOCK))
    select = (places == lane).astype(bf16)
    after = lane - places
    reached = after >= 0
    distance = jnp.maximum(after, 0).astype(f32)
    leave = jnp.clip(BLOCK - places, 0, BLOCK).astype(f32)
    for h in range(HEADS):
        c = head_cols(h)
        if h % 2 == 0:
            for fetch in fetches[2 * h : 2 * h + 4]:
                fetch.wait()
        chosen[:, c] = nn(select, v[:, c])
        weighted = q[:, c].astype(f32) * powers(rate[h], offset)
        state = decayed_state(weighted, grad[:, c])
        key = nn(select, k[:, c])
        table = jnp.where(reached, powers(rate[h], distance), 0.0)
        mixing = (nt(key.astype(bf16), q[:, c]) * table).astype(bf16)
        local = nn(mixing, grad[:, c])
        key = key * powers(rate[h], leave)
        for odd in range(2):
            i = 2 * h + odd
            out[i, 0:64] = state[64 * odd : 64 * odd + 64]
            out[i, 64:80] = key
            out[i, 80:96] = halves(local, chosen[:, c], odd)
        part = pl.ds(2 * h, 2)
        send = pltpu.make_async_copy(out.at[part], out_far.at[part], sent.at[h])
        send.start()
        sends.append(send)
    left = jnp.concatenate([chosen[...], ref[...], rot[...], jnp.zeros((2, WIDE), f32)], axis=0)
    right = jnp.concatenate(
        [proj[...] - rot[...], ref[...], rot[...], jnp.zeros((6, WIDE), f32)], axis=0
    )
    small[...] = jnp.zeros((24, 128), f32)
    small[:, 0:16] = full_nt(left, right)
    for send in sends:
        send.wait()


def inverse_of(small):
    g00, g01 = small[16:17, 4:5], small[16:17, 5:6]
    g10, g11 = small[17:18, 4:5], small[17:18, 5:6]
    det = g00 * g11 - g01 * g10
    return g11 / det, -g01 / det, -g10 / det, g00 / det


def third_terms(x):
    high = x.astype(bf16)
    rest = x - high.astype(f32)
    middle = rest.astype(bf16)
    low = (rest - middle.astype(f32)).astype(bf16)
    return jnp.concatenate([high, middle, low], axis=0)


def key_state(
    rate, positions, small, v, k, rot, ref, proj, bias, moved, state_far, basis, state, sent
):
    i00, i01, i10, i11 = inverse_of(small)
    c0, c1 = small[18:22, 4:5], small[18:22, 5:6]
    rotated = (
        rot[...]
        - (c0 * i00 + c1 * i10) * ref[0:1, :]
        - (c0 * i01 + c1 * i11) * ref[1:2, :]
    )
    lift = proj[...] - rotated
    rows = jnp.concatenate(
        [rotated, ref[...], lift, ref[...], jnp.zeros((4, WIDE), f32)], axis=0
    )
    turned = pltpu.roll(small[16:24, :], 122, 1)
    t0, t1 = turned[0:1], turned[1:2]
    full = (
        small[0:16, :]
        + bias[...]
        + small[0:16, 4:5] * (t0 * i00 + t1 * i10)
        + small[0:16, 5:6] * (t0 * i01 + t1 * i11)
    )
    full = jnp.where(cols_iota((NPOS, 128)) < 4, full, 0.0)
    shift = jnp.zeros((NPOS, WIDE), f32)
    for r in range(4):
        shift = shift + full[:, r : r + 1] * rotated[r : r + 1, :]
    select = selector(positions, block_start()).astype(bf16)
    select = jnp.concatenate([select, select, select], axis=0)
    shift = third_terms(shift)
    offset = rows_iota().astype(f32)
    sends = []
    for h in range(HEADS):
        c = head_cols(h)
        basis[h] = rows[:, c]
        new = (v[:, c].astype(f32) + tn(select, shift[:, c])).astype(bf16)
        moved[:, c] = new
        weighted = k[:, c].astype(f32) * powers(rate[h], BLOCK - 1.0 - offset)
        out = decayed_state(weighted, new)
        state[2 * h] = out[:64]
        state[2 * h + 1] = out[64:]
        part = pl.ds(2 * h, 2)
        send = pltpu.make_async_copy(state.at[part], state_far.at[part], sent.at[h])
        send.start()
        sends.append(send)
    for send in sends:
        send.wait()


def dot3(a, b):
    ah, al = split(a)
    bh, bl = split(b)
    return nt(ah, bh) + (nt(al, bh) + nt(ah, bl))


def backward_totals(rate, later, out, gathered):
    keep = powers(rate[near_place() // 2], jnp.full((64, 128), float(BLOCK), f32))
    keep_key = keep[0:NPOS]
    state = later[15, 0:64]
    key = later[0, 64:80]
    rows = later[15, 80:96]
    gathered[...] = jnp.zeros((NPOS, 128), f32)
    for b in range(14, -1, -1):
        gathered[:, 0:64] += dot3(later[b, 64:80], state)
        rows = rows + later[b, 80:96]
        state = state * keep + later[b, 0:64]
    for b in range(1, 16):
        key = key * keep_key + later[b, 64:80]
    out[0:64] = state
    out[64:80] = key
    out[80:96] = rows + gathered[...]


def backward_carried(
    rate, later, groups, basis, out_far, out, gathered, sent
):
    far, near = far_place(), near_place()
    exponent = jnp.full((64, 128), float(BLOCK), f32)
    keep = powers(rate[near // 2], exponent)
    keep_group = powers(rate[near // 2], exponent * 16.0)
    rows = groups[3, 80:96]
    gathered[...] = jnp.zeros((NPOS, 128), f32)
    carry = jnp.zeros((64, 128), f32)
    state = carry
    for z in (2, 1, 0):
        carry = carry * keep_group + groups[z + 1, 0:64]
        gathered[:, 0:64] += dot3(groups[z, 64:80], carry)
        rows = rows + groups[z, 80:96]
        state = jnp.where(far == z, carry, state)
    rows = rows + gathered[...]
    both = basis[near // 2]
    turned = pltpu.roll(both, 64, 1)
    odd = near % 2 == 1
    lane, row = cols_iota((16, 128)), rows_iota((16, 128))
    for_grad = jnp.where(odd, turned, both)
    for_value = jnp.where(odd, both, turned)
    right = jnp.where(
        row < 6,
        jnp.where(lane < 64, for_grad, 0.0),
        jnp.where(lane < 64, 0.0, for_value),
    )
    gathered[...] = jnp.zeros((NPOS, 128), f32)
    gathered[:, 0:16] = full_nt(rows, right)
    packed = gathered[0:8] + pltpu.roll(gathered[8:16], 16, 1)
    sends = []
    for b in range(15, -1, -1):
        out[b, 0:64] = state
        out[b, 64:72] = packed
        out[b, 72:88] = rows
        state = state * keep + later[b, 0:64]
        if b % 4 == 0:
            part = pl.ds(b, 4)
            send = pltpu.make_async_copy(out.at[part], out_far.at[part], sent.at[b // 4])
            send.start()
            sends.append(send)
    for send in sends:
        send.wait()


def forward_totals(rate, earlier, out):
    keep = powers(rate[near_place() // 2], jnp.full((64, 128), float(BLOCK), f32))
    state = earlier[0]
    for b in range(1, 16):
        state = state * keep + earlier[b]
    out[...] = state


def forward_carried(rate, earlier, one, two, three, out_far, out, sent):
    exponent = jnp.full((64, 128), float(BLOCK), f32)
    keep = powers(rate[near_place() // 2], exponent)
    keep_group = powers(rate[near_place() // 2], exponent * 16.0)
    state = (three[...] * keep_group + two[...]) * keep_group + one[...]
    sends = []
    for b in range(16):
        out[b] = state
        state = state * keep + earlier[b]
        if b % 4 == 3:
            part = pl.ds(b - 3, 4)
            send = pltpu.make_async_copy(out.at[part], out_far.at[part], sent.at[b // 4])
            send.start()
            sends.append(send)
    for send in sends:
        send.wait()


def sum_slices(x, out):
    total = x[0, 64:72]
    for i in range(1, 16):
        total = total + x[i, 64:72]
    lane = cols_iota((8, 128))
    out[0:8] = jnp.where(lane < 16, total, 0.0)
    out[8:16] = jnp.where(lane < 16, pltpu.roll(total, 112, 1), 0.0)


def products(head_sums, bias, x, parts):
    lane = cols_iota((NPOS, 128))
    sums = head_sums[...]
    turned = pltpu.roll(sums, 122, 1)
    code_grad = jnp.where(lane < 4, sums, 0.0)
    code = jnp.where(lane < 4, turned + bias[...], 0.0)
    both = code_grad + pltpu.roll(code, 4, 1)
    lane = cols_iota((4, 128))
    for i in range(16):
        got = full_tn(both, x[i, 72:88])
        parts[4 * i : 4 * i + 4] = jnp.where(lane < 64, got[4:8], got[0:4])
    along = (full_tn(code, sums) - full_tn(code_grad, turned))[0:4]
    total = jnp.broadcast_to(jnp.sum(code_grad, axis=0, keepdims=True), (4, 128))
    parts[64:68] = along
    parts[68:72] = total


def backward_rest(
    rate, positions, q, k, moved, grad, state, basis, head_sums, attended, grad_q, grad_k, grad_v
):
    between = rows_iota() - cols_iota()
    lower = between >= 0
    distance = jnp.maximum(between, 0).astype(f32)
    offset = rows_iota().astype(f32)
    select = selector(positions, block_start()).astype(bf16)
    select = jnp.concatenate([select, select, select], axis=0)
    code_grad = head_sums[...]
    for h in range(HEADS):
        c = head_cols(h)
        table = jnp.where(lower, powers(rate[h], distance), 0.0)
        leave = powers(rate[h], BLOCK - offset)
        high, low = split(jnp.concatenate([state[2 * h, 0:64], state[2 * h + 1, 0:64]], axis=0))
        qh, mh, kh, gh = q[:, c], moved[:, c], k[:, c], grad[:, c]
        mixing = (nt(qh, kh) * table).astype(bf16)
        grad_mixing = (nt(gh, mh) * table).astype(bf16)
        attended[:, c] = nn(mixing, mh)
        grad_q[:, c] = nn(grad_mixing, kh)
        inner = tn(grad_mixing, qh)
        grad_k[:, c] = (inner + leave * (nn(mh, high) + nn(mh, low))).astype(bf16)
        inner = tn(mixing, gh)
        lift = basis[h][6:10]
        fix = jnp.zeros((NPOS, SIZE), f32)
        for r in range(4):
            fix = fix + code_grad[:, r : r + 1] * lift[r : r + 1]
        out = inner + leave * (nt(kh, high) + nt(kh, low))
        grad_v[:, c] = (out + tn(select, third_terms(fix))).astype(bf16)


def forward_rest(
    rate, q, grad, state, attended_in, grad_q_in, small, ref, parts, others,
    attended, grad_q, grad_rotation, grad_weight, grad_bias,
):
    offset = rows_iota().astype(f32)
    i00, i01, i10, i11 = inverse_of(small)
    extra = parts[64:72] + others[64:72]
    a0, a1 = extra[0:4, 4:5], extra[0:4, 5:6]
    b0 = a0 * i00 + a1 * i10
    b1 = a0 * i01 + a1 * i11
    lane = cols_iota((4, 128))
    for h in range(HEADS):
        c = head_cols(h)
        enter = powers(rate[h], offset + 1.0)
        high, low = split(jnp.concatenate([state[2 * h], state[2 * h + 1]], axis=0))
        qh, gh = q[:, c], grad[:, c]
        attended[:, c] = (attended_in[:, c] + enter * (nt(qh, high) + nt(qh, low))).astype(bf16)
        grad_q[:, c] = (grad_q_in[:, c] + enter * (nn(gh, high) + nn(gh, low))).astype(bf16)
        both = parts[8 * h : 8 * h + 8] + others[8 * h : 8 * h + 8]
        turned = pltpu.roll(both, 64, 1)
        turn = jnp.where(lane < 64, both[0:4], turned[4:8])
        weight = jnp.where(lane < 64, turned[0:4], both[4:8])
        grad_weight[:, c] = weight
        grad_rotation[:, c] = turn - weight - b0 * ref[0:1, c] - b1 * ref[1:2, c]
    grad_bias[...] = extra[4, 0:4]


def call(kernel, specs, outs, scratch=(), far_outs=(), mib=8, flops=1e8, bytes_accessed=2e6):
    return pl.pallas_call(
        kernel,
        in_specs=[{"s": SMEM, "v": VMEM, "a": ANY}[s] for s in specs],
        out_specs=[ANY if n in far_outs else VMEM for n in range(len(outs))],
        out_shape=[jax.ShapeDtypeStruct(s, d) for s, d in outs],
        scratch_shapes=scratch,
        compiler_params=pltpu.CompilerParams(vmem_limit_bytes=mib * 1024 * 1024),
        cost_estimate=pl.CostEstimate(
            flops=int(flops), bytes_accessed=int(bytes_accessed), transcendentals=0
        ),
    )


def swap(x, axes):
    return lax.all_to_all(x, axes, 0, 0, tiled=False)


def ahead(x, d):
    return lax.ppermute(x, "zh", [(i, i + d) for i in range(4 - d)])


def shards(queries, key_rows, values, out_grad, rate, rotation, refusal, proj_weight, proj_bias, positions):
    q, k, v, grad = queries[0], key_rows[0], values[0], out_grad[0]
    ref = refusal.T
    bias = jnp.pad(proj_bias, (0, 124))[None, :]
    rows = (BLOCK, WIDE)
    tile = (NPOS, 128)

    def space(shape, dtype=f32):
        return pltpu.VMEM(shape, dtype)

    def marks(*shape):
        return pltpu.SemaphoreType.DMA(shape)

    grad_state, small = call(
        query_state,
        "ssaaaavvv",
        [((16, 96, 128), f32), ((24, 128), f32)],
        [space(rows, bf16)] * 4
        + [space((16, 96, 128)), space((NPOS, WIDE)), marks(4, 4), marks(HEADS)],
        (0,),
        mib=60,
    )(rate, positions, q, k, grad, v, rotation, ref, proj_weight)
    later = swap(grad_state, NEAR)
    small = lax.psum(small, "head")
    moved, state, basis = call(
        key_state,
        "ssvvvvvvv",
        [(rows, bf16), ((16, 64, 128), f32), ((HEADS, 16, 128), f32)],
        [space((16, 64, 128)), marks(HEADS)],
        (1,),
    )(rate, positions, small, v, k, rotation, ref, proj_weight, bias)
    state, later = lax.optimization_barrier((state, later))
    earlier = swap(state, NEAR)
    (own,) = call(backward_totals, "sv", [((96, 128), f32)], [space(tile)])(rate, later)
    groups = lax.all_gather(own, "zh")
    groups, earlier = lax.optimization_barrier((groups, earlier))
    (total,) = call(forward_totals, "sv", [((64, 128), f32)])(rate, earlier)
    passed = [ahead(total, d) for d in (2, 1, 3)]
    one, two, three = passed[1], passed[0], passed[2]
    (leaving,) = call(
        backward_carried,
        "svvv",
        [((16, 88, 128), f32)],
        [space((16, 88, 128)), space(tile), marks(4)],
        (0,),
    )(rate, later, groups, basis)
    leaving, total = lax.optimization_barrier((leaving, total))
    leaving = swap(leaving, NEAR)
    (entering,) = call(
        forward_carried,
        "svvvv",
        [((16, 64, 128), f32)],
        [space((16, 64, 128)), marks(4)],
        (0,),
    )(rate, earlier, one, two, three)
    (head_sums,) = call(sum_slices, "v", [(tile, f32)])(leaving)
    head_sums = lax.psum(head_sums, "head")
    entering, head_sums = lax.optimization_barrier((entering, head_sums))
    entering = swap(entering, NEAR)
    (parts,) = call(products, "vvv", [((72, 128), f32)])(head_sums, bias, leaving)
    others = lax.ppermute(parts, "dp", [(0, 1), (1, 0)])
    attended_in, grad_q_in, grad_k, grad_v = call(
        backward_rest, "ssvvvvvvv", [(rows, f32)] * 2 + [(rows, bf16)] * 2
    )(rate, positions, q, k, moved, grad, leaving, basis, head_sums)
    attended, grad_q, grad_rotation, grad_weight, grad_bias = call(
        forward_rest,
        "svvvvvvvvv",
        [(rows, bf16)] * 2 + [((4, WIDE), f32)] * 2 + [((4,), f32)],
    )(rate, q, grad, entering, attended_in, grad_q_in, small, ref, parts, others)
    return (
        attended[None],
        grad_q[None],
        grad_k[None],
        grad_v[None],
        grad_rotation,
        grad_weight,
        grad_bias,
    )


def solution(mesh):
    own = Mesh(mesh.devices.reshape(4, 4, 4, 4, 2), ("zh", "zl", "y", "head", "dp"))
    seq = ("zh", "zl", "y")
    stream = P("dp", seq, "head")
    return jax.shard_map(
        shards,
        mesh=own,
        in_specs=(
            stream,
            stream,
            stream,
            stream,
            P("head"),
            P(None, "head"),
            P("head", None),
            P(None, "head"),
            P(),
            P("dp", None),
        ),
        out_specs=(stream, stream, stream, stream, P(None, "head"), P(None, "head"), P()),
        check_vma=False,
    )
```

```python
import functools
import jax
import jax.numpy as jnp
from jax import lax
from jax.experimental import pallas as pl
from jax.experimental.pallas import tpu as pltpu
from jax.sharding import Mesh, PartitionSpec as P

highest = lax.Precision.HIGHEST
f32, bf16 = jnp.float32, jnp.bfloat16
BLOCK = 128
HEADS = 8
SIZE = 128
WIDE = HEADS * SIZE
NPOS = 16
NEAR = ("zl", "y")
ANY = pl.BlockSpec(memory_space=pltpu.HBM)
SMEM = pl.BlockSpec(memory_space=pltpu.SMEM)
VMEM = pl.BlockSpec(memory_space=pltpu.VMEM)


def nn(a, b):
    return lax.dot_general(a, b, (((1,), (0,)), ((), ())), preferred_element_type=f32)


def nt(a, b):
    return lax.dot_general(a, b, (((1,), (1,)), ((), ())), preferred_element_type=f32)


def tn(a, b):
    return lax.dot_general(a, b, (((0,), (0,)), ((), ())), preferred_element_type=f32)


def full_nt(a, b):
    return lax.dot_general(
        a, b, (((1,), (1,)), ((), ())), preferred_element_type=f32, precision=highest
    )


def full_tn(a, b):
    return lax.dot_general(
        a, b, (((0,), (0,)), ((), ())), preferred_element_type=f32, precision=highest
    )


def split(x):
    high = x.astype(bf16)
    return high, (x - high.astype(f32)).astype(bf16)


def log_keep(rate):
    total = jnp.float32(1.0 / 8.0)
    for n in range(7, 0, -1):
        total = total * rate + jnp.float32(1.0 / n)
    return -rate * total


def powers(logs, head, exponents):
    return jnp.exp(exponents * logs[pl.ds(head, 1), :])


def rows_iota(shape=(BLOCK, SIZE)):
    return lax.broadcasted_iota(jnp.int32, shape, 0)


def cols_iota(shape=(BLOCK, SIZE)):
    return lax.broadcasted_iota(jnp.int32, shape, 1)


def far_place():
    return lax.axis_index("zh")


def near_place():
    return lax.axis_index("zl") * 4 + lax.axis_index("y")


def block_start():
    return (far_place() * 16 + near_place()) * BLOCK


def local_places(positions, start):
    row = rows_iota((NPOS, BLOCK))
    wanted = jnp.full((NPOS, BLOCK), -1, jnp.int32)
    for j in range(NPOS):
        wanted = jnp.where(row == j, positions[0, j], wanted)
    return wanted - start


def selector(places):
    return (places[...] == cols_iota((NPOS, BLOCK))).astype(bf16)


def head_cols(h):
    return slice(h * SIZE, (h + 1) * SIZE)


def decayed_state(weighted, other):
    high, low = split(weighted)
    return tn(other, high) + tn(other, low)


def halves(left, right, odd):
    lane = cols_iota(left.shape)
    if odd:
        return jnp.where(lane < 64, pltpu.roll(left, 64, 1), right)
    return jnp.where(lane < 64, left, pltpu.roll(right, 64, 1))


def query_state(
    rate, positions, q_far, k_far, grad_far, v_far, rot, ref, proj,
    out_far, small, logs, places_out, q, k, grad, v, out, arrived, sent,
):
    fetches = []
    for n, (src, dst) in enumerate(((q_far, q), (grad_far, grad), (k_far, k), (v_far, v))):
        fetch = pltpu.make_async_copy(src, dst, arrived.at[n])
        fetch.start()
        fetches.append(fetch)
    sends = []

    def send(h, start, rows):
        here = (pl.ds(2 * h, 2), pl.ds(start, rows))
        copy = pltpu.make_async_copy(out.at[here], out_far.at[here], sent.at[len(sends)])
        copy.start()
        sends.append(copy)

    for h in range(HEADS):
        logs[h : h + 1, :] = jnp.full((1, 128), log_keep(rate[h]), f32)
    places = local_places(positions, block_start())
    places_out[...] = places
    lane = cols_iota((NPOS, BLOCK))
    select = (places == lane).astype(bf16)
    after = lane - places
    reached = after >= 0
    distance = jnp.maximum(after, 0).astype(f32)
    leave = jnp.clip(BLOCK - places, 0, BLOCK).astype(f32)
    tables = [jnp.where(reached, powers(logs, h, distance), 0.0) for h in range(HEADS)]
    offset = rows_iota().astype(f32)
    for fetch in fetches[:2]:
        fetch.wait()
    for h in range(HEADS):
        c = head_cols(h)
        weighted = q[:, c].astype(f32) * powers(logs, h, offset)
        state = decayed_state(weighted, grad[:, c])
        out[2 * h, 0:64] = state[:64]
        out[2 * h + 1, 0:64] = state[64:]
        send(h, 0, 64)
    for fetch in fetches[2:]:
        fetch.wait()
    keys = nn(select, k[...])
    chosen = nn(select, v[...])
    low = keys.astype(bf16)
    scores = [nt(low[:, head_cols(h)], q[:, head_cols(h)]) for h in range(HEADS)]
    mixing = [(scores[h] * tables[h]).astype(bf16) for h in range(HEADS)]
    local = [nn(mixing[h], grad[:, head_cols(h)]) for h in range(HEADS)]
    for h in range(HEADS):
        c = head_cols(h)
        key = keys[:, c] * powers(logs, h, leave)
        for odd in range(2):
            i = 2 * h + odd
            out[i, 64:80] = key
            out[i, 80:96] = halves(local[h], chosen[:, c], odd)
        send(h, 64, 32)
    left = jnp.concatenate([chosen, ref[...], rot[...], jnp.zeros((2, WIDE), f32)], axis=0)
    right = jnp.concatenate(
        [proj[...] - rot[...], ref[...], rot[...], jnp.zeros((6, WIDE), f32)], axis=0
    )
    small[...] = jnp.zeros((24, 128), f32)
    small[:, 0:16] = full_nt(left, right)
    for copy in sends:
        copy.wait()


def inverse_of(small):
    g00, g01 = small[16:17, 4:5], small[16:17, 5:6]
    g10, g11 = small[17:18, 4:5], small[17:18, 5:6]
    det = g00 * g11 - g01 * g10
    return g11 / det, -g01 / det, -g10 / det, g00 / det


def third_terms(x):
    high = x.astype(bf16)
    rest = x - high.astype(f32)
    middle = rest.astype(bf16)
    low = (rest - middle.astype(f32)).astype(bf16)
    return jnp.concatenate([high, middle, low], axis=0)


def key_state(
    logs, places, small, v, k, rot, ref, proj, bias, moved, state_far, basis, state, sent
):
    i00, i01, i10, i11 = inverse_of(small)
    c0, c1 = small[18:22, 4:5], small[18:22, 5:6]
    rotated = (
        rot[...]
        - (c0 * i00 + c1 * i10) * ref[0:1, :]
        - (c0 * i01 + c1 * i11) * ref[1:2, :]
    )
    lift = proj[...] - rotated
    rows = jnp.concatenate(
        [rotated, ref[...], lift, ref[...], jnp.zeros((4, WIDE), f32)], axis=0
    )
    turned = pltpu.roll(small[16:24, :], 122, 1)
    t0, t1 = turned[0:1], turned[1:2]
    full = (
        small[0:16, :]
        + bias[...]
        + small[0:16, 4:5] * (t0 * i00 + t1 * i10)
        + small[0:16, 5:6] * (t0 * i01 + t1 * i11)
    )
    full = jnp.where(cols_iota((NPOS, 128)) < 4, full, 0.0)
    shift = jnp.zeros((NPOS, WIDE), f32)
    for r in range(4):
        shift = shift + full[:, r : r + 1] * rotated[r : r + 1, :]
    select = selector(places)
    select = jnp.concatenate([select, select, select], axis=0)
    shift = third_terms(shift)
    offset = rows_iota().astype(f32)
    sends = []
    for h in range(HEADS):
        c = head_cols(h)
        basis[h] = rows[:, c]
        new = (v[:, c].astype(f32) + tn(select, shift[:, c])).astype(bf16)
        moved[:, c] = new
        weighted = k[:, c].astype(f32) * powers(logs, h, BLOCK - 1.0 - offset)
        out = decayed_state(weighted, new)
        state[2 * h] = out[:64]
        state[2 * h + 1] = out[64:]
        part = pl.ds(2 * h, 2)
        send = pltpu.make_async_copy(state.at[part], state_far.at[part], sent.at[h])
        send.start()
        sends.append(send)
    for send in sends:
        send.wait()


def dot3(a, b):
    ah, al = split(a)
    bh, bl = split(b)
    return nt(ah, bh) + (nt(al, bh) + nt(ah, bl))


def backward_totals(logs, later, out, gathered):
    keep = powers(logs, near_place() // 2, jnp.full((64, 128), float(BLOCK), f32))
    keep_key = keep[0:NPOS]
    state = later[15, 0:64]
    key = later[0, 64:80]
    rows = later[15, 80:96]
    gathered[...] = jnp.zeros((NPOS, 128), f32)
    for b in range(14, -1, -1):
        gathered[:, 0:64] += dot3(later[b, 64:80], state)
        rows = rows + later[b, 80:96]
        state = state * keep + later[b, 0:64]
    for b in range(1, 16):
        key = key * keep_key + later[b, 64:80]
    out[0:64] = state
    out[64:80] = key
    out[80:96] = rows + gathered[...]


def backward_carried(
    logs, later, groups, basis, out_far, out, gathered, sent
):
    far, near = far_place(), near_place()
    exponent = jnp.full((64, 128), float(BLOCK), f32)
    keep = powers(logs, near // 2, exponent)
    keep_group = powers(logs, near // 2, exponent * 16.0)
    rows = groups[3, 80:96]
    gathered[...] = jnp.zeros((NPOS, 128), f32)
    carry = jnp.zeros((64, 128), f32)
    state = carry
    for z in (2, 1, 0):
        carry = carry * keep_group + groups[z + 1, 0:64]
        gathered[:, 0:64] += dot3(groups[z, 64:80], carry)
        rows = rows + groups[z, 80:96]
        state = jnp.where(far == z, carry, state)
    rows = rows + gathered[...]
    both = basis[near // 2]
    turned = pltpu.roll(both, 64, 1)
    odd = near % 2 == 1
    lane, row = cols_iota((16, 128)), rows_iota((16, 128))
    for_grad = jnp.where(odd, turned, both)
    for_value = jnp.where(odd, both, turned)
    right = jnp.where(
        row < 6,
        jnp.where(lane < 64, for_grad, 0.0),
        jnp.where(lane < 64, 0.0, for_value),
    )
    gathered[...] = jnp.zeros((NPOS, 128), f32)
    gathered[:, 0:16] = full_nt(rows, right)
    packed = gathered[0:8] + pltpu.roll(gathered[8:16], 16, 1)
    sends = []
    for b in range(15, -1, -1):
        out[b, 0:64] = state
        out[b, 64:72] = packed
        out[b, 72:88] = rows
        state = state * keep + later[b, 0:64]
        if b % 4 == 0:
            part = pl.ds(b, 4)
            send = pltpu.make_async_copy(out.at[part], out_far.at[part], sent.at[b // 4])
            send.start()
            sends.append(send)
    for send in sends:
        send.wait()


def forward_totals(logs, earlier, out):
    keep = powers(logs, near_place() // 2, jnp.full((64, 128), float(BLOCK), f32))
    state = earlier[0]
    for b in range(1, 16):
        state = state * keep + earlier[b]
    out[...] = state


def forward_carried(logs, earlier, one, two, three, out_far, out, sent):
    exponent = jnp.full((64, 128), float(BLOCK), f32)
    keep = powers(logs, near_place() // 2, exponent)
    keep_group = powers(logs, near_place() // 2, exponent * 16.0)
    state = (three[...] * keep_group + two[...]) * keep_group + one[...]
    sends = []
    for b in range(16):
        out[b] = state
        state = state * keep + earlier[b]
        if b % 4 == 3:
            part = pl.ds(b - 3, 4)
            send = pltpu.make_async_copy(out.at[part], out_far.at[part], sent.at[b // 4])
            send.start()
            sends.append(send)
    for send in sends:
        send.wait()


def sum_slices(x, out):
    total = x[0, 64:72]
    for i in range(1, 16):
        total = total + x[i, 64:72]
    lane = cols_iota((8, 128))
    out[0:8] = jnp.where(lane < 16, total, 0.0)
    out[8:16] = jnp.where(lane < 16, pltpu.roll(total, 112, 1), 0.0)


def products(head_sums, bias, x, parts):
    lane = cols_iota((NPOS, 128))
    sums = head_sums[...]
    turned = pltpu.roll(sums, 122, 1)
    code_grad = jnp.where(lane < 4, sums, 0.0)
    code = jnp.where(lane < 4, turned + bias[...], 0.0)
    both = code_grad + pltpu.roll(code, 4, 1)
    lane = cols_iota((4, 128))
    for i in range(16):
        got = full_tn(both, x[i, 72:88])
        parts[4 * i : 4 * i + 4] = jnp.where(lane < 64, got[4:8], got[0:4])
    along = (full_tn(code, sums) - full_tn(code_grad, turned))[0:4]
    total = jnp.broadcast_to(jnp.sum(code_grad, axis=0, keepdims=True), (4, 128))
    parts[64:68] = along
    parts[68:72] = total


def backward_rest(
    logs, places, q, k, moved, grad, state, basis, head_sums, attended, grad_q, grad_k, grad_v
):
    between = rows_iota() - cols_iota()
    lower = between >= 0
    distance = jnp.maximum(between, 0).astype(f32)
    offset = rows_iota().astype(f32)
    select = selector(places)
    select = jnp.concatenate([select, select, select], axis=0)
    code_grad = head_sums[...]
    for h in range(HEADS):
        c = head_cols(h)
        table = jnp.where(lower, powers(logs, h, distance), 0.0)
        leave = powers(logs, h, BLOCK - offset)
        high, low = split(jnp.concatenate([state[2 * h, 0:64], state[2 * h + 1, 0:64]], axis=0))
        qh, mh, kh, gh = q[:, c], moved[:, c], k[:, c], grad[:, c]
        mixing = (nt(qh, kh) * table).astype(bf16)
        grad_mixing = (nt(gh, mh) * table).astype(bf16)
        attended[:, c] = nn(mixing, mh)
        grad_q[:, c] = nn(grad_mixing, kh)
        inner = tn(grad_mixing, qh)
        grad_k[:, c] = (inner + leave * (nn(mh, high) + nn(mh, low))).astype(bf16)
        inner = tn(mixing, gh)
        lift = basis[h][6:10]
        fix = jnp.zeros((NPOS, SIZE), f32)
        for r in range(4):
            fix = fix + code_grad[:, r : r + 1] * lift[r : r + 1]
        out = inner + leave * (nt(kh, high) + nt(kh, low))
        grad_v[:, c] = (out + tn(select, third_terms(fix))).astype(bf16)


def forward_rest(
    logs, q, grad, state, attended_in, grad_q_in, small, ref, parts, others,
    attended_far, grad_q_far, grad_rotation, grad_weight, grad_bias, attended, grad_q, sent,
):
    sends = []
    offset = rows_iota().astype(f32)
    i00, i01, i10, i11 = inverse_of(small)
    extra = parts[64:72] + others[64:72]
    a0, a1 = extra[0:4, 4:5], extra[0:4, 5:6]
    b0 = a0 * i00 + a1 * i10
    b1 = a0 * i01 + a1 * i11
    lane = cols_iota((4, 128))
    for h in range(HEADS):
        c = head_cols(h)
        enter = powers(logs, h, offset + 1.0)
        high, low = split(jnp.concatenate([state[2 * h], state[2 * h + 1]], axis=0))
        qh, gh = q[:, c], grad[:, c]
        attended[:, c] = (attended_in[:, c] + enter * (nt(qh, high) + nt(qh, low))).astype(bf16)
        grad_q[:, c] = (grad_q_in[:, c] + enter * (nn(gh, high) + nn(gh, low))).astype(bf16)
        if h % 2 == 1:
            wide = slice((h - 1) * SIZE, (h + 1) * SIZE)
            pairs = ((attended, attended_far), (grad_q, grad_q_far))
            for n, (src, dst) in enumerate(pairs):
                copy = pltpu.make_async_copy(src.at[:, wide], dst.at[:, wide], sent.at[h // 2, n])
                copy.start()
                sends.append(copy)
        both = parts[8 * h : 8 * h + 8] + others[8 * h : 8 * h + 8]
        turned = pltpu.roll(both, 64, 1)
        turn = jnp.where(lane < 64, both[0:4], turned[4:8])
        weight = jnp.where(lane < 64, turned[0:4], both[4:8])
        grad_weight[:, c] = weight
        grad_rotation[:, c] = turn - weight - b0 * ref[0:1, c] - b1 * ref[1:2, c]
    grad_bias[...] = extra[4, 0:4]
    for copy in sends:
        copy.wait()


def call(kernel, specs, outs, scratch=(), far_outs=(), mib=8, flops=1e8, bytes_accessed=2e6):
    return pl.pallas_call(
        kernel,
        in_specs=[{"s": SMEM, "v": VMEM, "a": ANY}[s] for s in specs],
        out_specs=[ANY if n in far_outs else VMEM for n in range(len(outs))],
        out_shape=[jax.ShapeDtypeStruct(s, d) for s, d in outs],
        scratch_shapes=scratch,
        compiler_params=pltpu.CompilerParams(vmem_limit_bytes=mib * 1024 * 1024),
        cost_estimate=pl.CostEstimate(
            flops=int(flops), bytes_accessed=int(bytes_accessed), transcendentals=0
        ),
    )


def swap(x, axes):
    return lax.all_to_all(x, axes, 0, 0, tiled=False)


def ahead(x, d):
    return lax.ppermute(x, "zh", [(i, i + d) for i in range(4 - d)])


def shards(queries, key_rows, values, out_grad, rate, rotation, refusal, proj_weight, proj_bias, positions):
    q, k, v, grad = queries[0], key_rows[0], values[0], out_grad[0]
    ref = refusal.T
    bias = jnp.pad(proj_bias, (0, 124))[None, :]
    rows = (BLOCK, WIDE)
    tile = (NPOS, 128)

    def space(shape, dtype=f32):
        return pltpu.VMEM(shape, dtype)

    def marks(*shape):
        return pltpu.SemaphoreType.DMA(shape)

    grad_state, small, logs, places = call(
        query_state,
        "ssaaaavvv",
        [((16, 96, 128), f32), ((24, 128), f32), ((8, 128), f32), (tile, jnp.int32)],
        [space(rows, bf16)] * 4 + [space((16, 96, 128)), marks(4), marks(2 * HEADS)],
        (0,),
        mib=60,
    )(rate, positions, q, k, grad, v, rotation, ref, proj_weight)
    later = swap(grad_state, NEAR)
    small = lax.psum(small, "head")
    moved, state, basis = call(
        key_state,
        "vvvvvvvvv",
        [(rows, bf16), ((16, 64, 128), f32), ((HEADS, 16, 128), f32)],
        [space((16, 64, 128)), marks(HEADS)],
        (1,),
    )(logs, places, small, v, k, rotation, ref, proj_weight, bias)
    state, later = lax.optimization_barrier((state, later))
    earlier = swap(state, NEAR)
    (own,) = call(backward_totals, "vv", [((96, 128), f32)], [space(tile)])(logs, later)
    groups = lax.all_gather(own, "zh")
    groups, earlier = lax.optimization_barrier((groups, earlier))
    (total,) = call(forward_totals, "vv", [((64, 128), f32)])(logs, earlier)
    passed = [ahead(total, d) for d in (2, 1, 3)]
    one, two, three = passed[1], passed[0], passed[2]
    (leaving,) = call(
        backward_carried,
        "vvvv",
        [((16, 88, 128), f32)],
        [space((16, 88, 128)), space(tile), marks(4)],
        (0,),
    )(logs, later, groups, basis)
    leaving, total = lax.optimization_barrier((leaving, total))
    leaving = swap(leaving, NEAR)
    (entering,) = call(
        forward_carried,
        "vvvvv",
        [((16, 64, 128), f32)],
        [space((16, 64, 128)), marks(4)],
        (0,),
    )(logs, earlier, one, two, three)
    (head_sums,) = call(sum_slices, "v", [(tile, f32)])(leaving)
    head_sums = lax.psum(head_sums, "head")
    entering, head_sums = lax.optimization_barrier((entering, head_sums))
    entering = swap(entering, NEAR)
    (parts,) = call(products, "vvv", [((72, 128), f32)])(head_sums, bias, leaving)
    others = lax.ppermute(parts, "dp", [(0, 1), (1, 0)])
    attended_in, grad_q_in, grad_k, grad_v = call(
        backward_rest, "vvvvvvvvv", [(rows, f32)] * 2 + [(rows, bf16)] * 2
    )(logs, places, q, k, moved, grad, leaving, basis, head_sums)
    attended, grad_q, grad_rotation, grad_weight, grad_bias = call(
        forward_rest,
        "vvvvvvvvvv",
        [(rows, bf16)] * 2 + [((4, WIDE), f32)] * 2 + [((4,), f32)],
        [space(rows, bf16)] * 2 + [marks(4, 2)],
        (0, 1),
    )(logs, q, grad, entering, attended_in, grad_q_in, small, ref, parts, others)
    return (
        attended[None],
        grad_q[None],
        grad_k[None],
        grad_v[None],
        grad_rotation,
        grad_weight,
        grad_bias,
    )


def solution(mesh):
    own = Mesh(mesh.devices.reshape(4, 4, 4, 4, 2), ("zh", "zl", "y", "head", "dp"))
    seq = ("zh", "zl", "y")
    stream = P("dp", seq, "head")
    return jax.shard_map(
        shards,
        mesh=own,
        in_specs=(
            stream,
            stream,
            stream,
            stream,
            P("head"),
            P(None, "head"),
            P("head", None),
            P(None, "head"),
            P(),
            P("dp", None),
        ),
        out_specs=(stream, stream, stream, stream, P(None, "head"), P(None, "head"), P()),
        check_vma=False,
    )
```

```python
import functools
import jax
import jax.numpy as jnp
from jax import lax
from jax.experimental import pallas as pl
from jax.experimental.pallas import tpu as pltpu
from jax.sharding import Mesh, PartitionSpec as P

highest = lax.Precision.HIGHEST
f32, bf16 = jnp.float32, jnp.bfloat16
BLOCK = 128
HEADS = 8
SIZE = 128
WIDE = HEADS * SIZE
NPOS = 16
NEAR = ("zl", "y")
ANY = pl.BlockSpec(memory_space=pltpu.HBM)
SMEM = pl.BlockSpec(memory_space=pltpu.SMEM)
VMEM = pl.BlockSpec(memory_space=pltpu.VMEM)


def nn(a, b):
    return lax.dot_general(a, b, (((1,), (0,)), ((), ())), preferred_element_type=f32)


def nt(a, b):
    return lax.dot_general(a, b, (((1,), (1,)), ((), ())), preferred_element_type=f32)


def tn(a, b):
    return lax.dot_general(a, b, (((0,), (0,)), ((), ())), preferred_element_type=f32)


def full_nt(a, b):
    return lax.dot_general(
        a, b, (((1,), (1,)), ((), ())), preferred_element_type=f32, precision=highest
    )


def full_tn(a, b):
    return lax.dot_general(
        a, b, (((0,), (0,)), ((), ())), preferred_element_type=f32, precision=highest
    )


def split(x):
    high = x.astype(bf16)
    return high, (x - high.astype(f32)).astype(bf16)


def log_keep(rate):
    total = jnp.float32(1.0 / 8.0)
    for n in range(7, 0, -1):
        total = total * rate + jnp.float32(1.0 / n)
    return -rate * total


def powers(logs, head, exponents):
    return jnp.exp(exponents * logs[pl.ds(head, 1), :])


def rows_iota(shape=(BLOCK, SIZE)):
    return lax.broadcasted_iota(jnp.int32, shape, 0)


def cols_iota(shape=(BLOCK, SIZE)):
    return lax.broadcasted_iota(jnp.int32, shape, 1)


def far_place():
    return lax.axis_index("zh")


def near_place():
    return lax.axis_index("zl") * 4 + lax.axis_index("y")


def block_start():
    return (far_place() * 16 + near_place()) * BLOCK


def local_places(positions, start):
    row = rows_iota((NPOS, BLOCK))
    wanted = jnp.full((NPOS, BLOCK), -1, jnp.int32)
    for j in range(NPOS):
        wanted = jnp.where(row == j, positions[0, j], wanted)
    return wanted - start


def selector(places):
    return (places[...] == cols_iota((NPOS, BLOCK))).astype(bf16)


def head_cols(h):
    return slice(h * SIZE, (h + 1) * SIZE)


def decayed_state(weighted, other):
    high, low = split(weighted)
    return tn(other, high) + tn(other, low)


def halves(left, right, odd):
    lane = cols_iota(left.shape)
    if odd:
        return jnp.where(lane < 64, pltpu.roll(left, 64, 1), right)
    return jnp.where(lane < 64, left, pltpu.roll(right, 64, 1))


def query_state(
    rate, positions, q_far, k_far, grad_far, v_far, rot, ref, proj,
    out_far, small, logs, places_out, q, k, grad, v, out, arrived, sent,
):
    fetches = []
    for n, (src, dst) in enumerate(((q_far, q), (grad_far, grad), (k_far, k), (v_far, v))):
        fetch = pltpu.make_async_copy(src, dst, arrived.at[n])
        fetch.start()
        fetches.append(fetch)
    sends = []

    def send(h, start, rows):
        here = (pl.ds(2 * h, 2), pl.ds(start, rows))
        copy = pltpu.make_async_copy(out.at[here], out_far.at[here], sent.at[len(sends)])
        copy.start()
        sends.append(copy)

    for h in range(HEADS):
        logs[h : h + 1, :] = jnp.full((1, 128), log_keep(rate[h]), f32)
    places = local_places(positions, block_start())
    places_out[...] = places
    lane = cols_iota((NPOS, BLOCK))
    select = (places == lane).astype(bf16)
    after = lane - places
    reached = after >= 0
    distance = jnp.maximum(after, 0).astype(f32)
    leave = jnp.clip(BLOCK - places, 0, BLOCK).astype(f32)
    tables = [jnp.where(reached, powers(logs, h, distance), 0.0) for h in range(HEADS)]
    offset = rows_iota().astype(f32)
    for fetch in fetches[:2]:
        fetch.wait()
    for h in range(HEADS):
        c = head_cols(h)
        weighted = q[:, c].astype(f32) * powers(logs, h, offset)
        state = decayed_state(weighted, grad[:, c])
        out[2 * h, 0:64] = state[:64]
        out[2 * h + 1, 0:64] = state[64:]
        send(h, 0, 64)
    for fetch in fetches[2:]:
        fetch.wait()
    keys = nn(select, k[...])
    chosen = nn(select, v[...])
    low = keys.astype(bf16)
    scores = [nt(low[:, head_cols(h)], q[:, head_cols(h)]) for h in range(HEADS)]
    mixing = [(scores[h] * tables[h]).astype(bf16) for h in range(HEADS)]
    local = [nn(mixing[h], grad[:, head_cols(h)]) for h in range(HEADS)]
    for h in range(HEADS):
        c = head_cols(h)
        key = keys[:, c] * powers(logs, h, leave)
        for odd in range(2):
            i = 2 * h + odd
            out[i, 64:80] = key
            out[i, 80:96] = halves(local[h], chosen[:, c], odd)
        send(h, 64, 32)
    left = jnp.concatenate([chosen, ref[...], rot[...], jnp.zeros((2, WIDE), f32)], axis=0)
    right = jnp.concatenate(
        [proj[...] - rot[...], ref[...], rot[...], jnp.zeros((6, WIDE), f32)], axis=0
    )
    small[...] = jnp.zeros((24, 128), f32)
    small[:, 0:16] = full_nt(left, right)
    for copy in sends:
        copy.wait()


def inverse_of(small):
    g00, g01 = small[16:17, 4:5], small[16:17, 5:6]
    g10, g11 = small[17:18, 4:5], small[17:18, 5:6]
    det = g00 * g11 - g01 * g10
    return g11 / det, -g01 / det, -g10 / det, g00 / det


def third_terms(x):
    high = x.astype(bf16)
    rest = x - high.astype(f32)
    middle = rest.astype(bf16)
    low = (rest - middle.astype(f32)).astype(bf16)
    return jnp.concatenate([high, middle, low], axis=0)


def key_state(
    logs, places, small, v, k, rot, ref, proj, bias, moved, state_far, basis, state, sent
):
    i00, i01, i10, i11 = inverse_of(small)
    c0, c1 = small[18:22, 4:5], small[18:22, 5:6]
    rotated = (
        rot[...]
        - (c0 * i00 + c1 * i10) * ref[0:1, :]
        - (c0 * i01 + c1 * i11) * ref[1:2, :]
    )
    lift = proj[...] - rotated
    rows = jnp.concatenate(
        [rotated, ref[...], lift, ref[...], jnp.zeros((4, WIDE), f32)], axis=0
    )
    turned = pltpu.roll(small[16:24, :], 122, 1)
    t0, t1 = turned[0:1], turned[1:2]
    full = (
        small[0:16, :]
        + bias[...]
        + small[0:16, 4:5] * (t0 * i00 + t1 * i10)
        + small[0:16, 5:6] * (t0 * i01 + t1 * i11)
    )
    full = jnp.where(cols_iota((NPOS, 128)) < 4, full, 0.0)
    shift = jnp.zeros((NPOS, WIDE), f32)
    for r in range(4):
        shift = shift + full[:, r : r + 1] * rotated[r : r + 1, :]
    select = selector(places)
    select = jnp.concatenate([select, select, select], axis=0)
    shift = third_terms(shift)
    offset = rows_iota().astype(f32)
    sends = []
    for h in range(HEADS):
        c = head_cols(h)
        basis[h] = rows[:, c]
        new = (v[:, c].astype(f32) + tn(select, shift[:, c])).astype(bf16)
        moved[:, c] = new
        weighted = k[:, c].astype(f32) * powers(logs, h, BLOCK - 1.0 - offset)
        out = decayed_state(weighted, new)
        state[2 * h] = out[:64]
        state[2 * h + 1] = out[64:]
        part = pl.ds(2 * h, 2)
        send = pltpu.make_async_copy(state.at[part], state_far.at[part], sent.at[h])
        send.start()
        sends.append(send)
    for send in sends:
        send.wait()


def dot3(a, b):
    ah, al = split(a)
    bh, bl = split(b)
    return nt(ah, bh) + (nt(al, bh) + nt(ah, bl))


def backward_totals(logs, later, out, gathered):
    keep = powers(logs, near_place() // 2, jnp.full((64, 128), float(BLOCK), f32))
    keep_key = keep[0:NPOS]
    state = later[15, 0:64]
    key = later[0, 64:80]
    rows = later[15, 80:96]
    gathered[...] = jnp.zeros((NPOS, 128), f32)
    for b in range(14, -1, -1):
        gathered[:, 0:64] += dot3(later[b, 64:80], state)
        rows = rows + later[b, 80:96]
        state = state * keep + later[b, 0:64]
    for b in range(1, 16):
        key = key * keep_key + later[b, 64:80]
    out[0:64] = state
    out[64:80] = key
    out[80:96] = rows + gathered[...]


def backward_carried(
    logs, later, groups, basis, out_far, out, gathered, sent
):
    far, near = far_place(), near_place()
    exponent = jnp.full((64, 128), float(BLOCK), f32)
    keep = powers(logs, near // 2, exponent)
    keep_group = powers(logs, near // 2, exponent * 16.0)
    rows = groups[3, 80:96]
    gathered[...] = jnp.zeros((NPOS, 128), f32)
    carry = jnp.zeros((64, 128), f32)
    state = carry
    for z in (2, 1, 0):
        carry = carry * keep_group + groups[z + 1, 0:64]
        gathered[:, 0:64] += dot3(groups[z, 64:80], carry)
        rows = rows + groups[z, 80:96]
        state = jnp.where(far == z, carry, state)
    rows = rows + gathered[...]
    both = basis[near // 2]
    turned = pltpu.roll(both, 64, 1)
    odd = near % 2 == 1
    lane, row = cols_iota((16, 128)), rows_iota((16, 128))
    for_grad = jnp.where(odd, turned, both)
    for_value = jnp.where(odd, both, turned)
    right = jnp.where(
        row < 6,
        jnp.where(lane < 64, for_grad, 0.0),
        jnp.where(lane < 64, 0.0, for_value),
    )
    gathered[...] = jnp.zeros((NPOS, 128), f32)
    gathered[:, 0:16] = full_nt(rows, right)
    packed = gathered[0:8] + pltpu.roll(gathered[8:16], 16, 1)
    sends = []
    for b in range(15, -1, -1):
        out[b, 0:64] = state
        out[b, 64:72] = packed
        out[b, 72:88] = rows
        state = state * keep + later[b, 0:64]
        if b % 4 == 0:
            part = pl.ds(b, 4)
            send = pltpu.make_async_copy(out.at[part], out_far.at[part], sent.at[b // 4])
            send.start()
            sends.append(send)
    for send in sends:
        send.wait()


def forward_totals(logs, earlier, out):
    keep = powers(logs, near_place() // 2, jnp.full((64, 128), float(BLOCK), f32))
    state = earlier[0]
    for b in range(1, 16):
        state = state * keep + earlier[b]
    out[...] = state


def forward_carried(logs, earlier, one, two, three, out_far, out, sent):
    exponent = jnp.full((64, 128), float(BLOCK), f32)
    keep = powers(logs, near_place() // 2, exponent)
    keep_group = powers(logs, near_place() // 2, exponent * 16.0)
    state = (three[...] * keep_group + two[...]) * keep_group + one[...]
    sends = []
    for b in range(16):
        out[b] = state
        state = state * keep + earlier[b]
        if b % 4 == 3:
            part = pl.ds(b - 3, 4)
            send = pltpu.make_async_copy(out.at[part], out_far.at[part], sent.at[b // 4])
            send.start()
            sends.append(send)
    for send in sends:
        send.wait()


def sum_slices(x, out):
    total = x[0, 64:72]
    for i in range(1, 16):
        total = total + x[i, 64:72]
    lane = cols_iota((8, 128))
    out[0:8] = jnp.where(lane < 16, total, 0.0)
    out[8:16] = jnp.where(lane < 16, pltpu.roll(total, 112, 1), 0.0)


def products(head_sums, bias, x, parts):
    lane = cols_iota((NPOS, 128))
    sums = head_sums[...]
    turned = pltpu.roll(sums, 122, 1)
    code_grad = jnp.where(lane < 4, sums, 0.0)
    code = jnp.where(lane < 4, turned + bias[...], 0.0)
    both = code_grad + pltpu.roll(code, 4, 1)
    lane = cols_iota((4, 128))
    for i in range(16):
        got = full_tn(both, x[i, 72:88])
        parts[4 * i : 4 * i + 4] = jnp.where(lane < 64, got[4:8], got[0:4])
    along = (full_tn(code, sums) - full_tn(code_grad, turned))[0:4]
    total = jnp.broadcast_to(jnp.sum(code_grad, axis=0, keepdims=True), (4, 128))
    parts[64:68] = along
    parts[68:72] = total


def backward_rest(
    logs, places, q, k, moved, grad, state, basis, head_sums, attended, grad_q, grad_k, grad_v
):
    between = rows_iota() - cols_iota()
    lower = between >= 0
    distance = jnp.maximum(between, 0).astype(f32)
    offset = rows_iota().astype(f32)
    select = selector(places)
    select = jnp.concatenate([select, select, select], axis=0)
    code_grad = head_sums[...]
    for h in range(HEADS):
        c = head_cols(h)
        table = jnp.where(lower, powers(logs, h, distance), 0.0)
        leave = powers(logs, h, BLOCK - offset)
        high, low = split(jnp.concatenate([state[2 * h, 0:64], state[2 * h + 1, 0:64]], axis=0))
        qh, mh, kh, gh = q[:, c], moved[:, c], k[:, c], grad[:, c]
        mixing = (nt(qh, kh) * table).astype(bf16)
        grad_mixing = (nt(gh, mh) * table).astype(bf16)
        attended[:, c] = nn(mixing, mh)
        grad_q[:, c] = nn(grad_mixing, kh)
        inner = tn(grad_mixing, qh)
        grad_k[:, c] = (inner + leave * (nn(mh, high) + nn(mh, low))).astype(bf16)
        inner = tn(mixing, gh)
        lift = basis[h][6:10]
        fix = jnp.zeros((NPOS, SIZE), f32)
        for r in range(4):
            fix = fix + code_grad[:, r : r + 1] * lift[r : r + 1]
        out = inner + leave * (nt(kh, high) + nt(kh, low))
        grad_v[:, c] = (out + tn(select, third_terms(fix))).astype(bf16)


def forward_rest(
    logs, q, grad, state, attended_in, grad_q_in, small, ref, parts, others,
    attended_far, grad_q_far, grad_rotation, grad_weight, grad_bias, attended, grad_q, sent,
):
    sends = []
    offset = rows_iota().astype(f32)
    i00, i01, i10, i11 = inverse_of(small)
    extra = parts[64:72] + others[64:72]
    a0, a1 = extra[0:4, 4:5], extra[0:4, 5:6]
    b0 = a0 * i00 + a1 * i10
    b1 = a0 * i01 + a1 * i11
    lane = cols_iota((4, 128))
    for h in range(HEADS):
        c = head_cols(h)
        enter = powers(logs, h, offset + 1.0)
        high, low = split(jnp.concatenate([state[2 * h], state[2 * h + 1]], axis=0))
        qh, gh = q[:, c], grad[:, c]
        attended[:, c] = (attended_in[:, c] + enter * (nt(qh, high) + nt(qh, low))).astype(bf16)
        grad_q[:, c] = (grad_q_in[:, c] + enter * (nn(gh, high) + nn(gh, low))).astype(bf16)
        if h % 2 == 1:
            wide = slice((h - 1) * SIZE, (h + 1) * SIZE)
            pairs = ((attended, attended_far), (grad_q, grad_q_far))
            for n, (src, dst) in enumerate(pairs):
                copy = pltpu.make_async_copy(src.at[:, wide], dst.at[:, wide], sent.at[h // 2, n])
                copy.start()
                sends.append(copy)
        both = parts[8 * h : 8 * h + 8] + others[8 * h : 8 * h + 8]
        turned = pltpu.roll(both, 64, 1)
        turn = jnp.where(lane < 64, both[0:4], turned[4:8])
        weight = jnp.where(lane < 64, turned[0:4], both[4:8])
        grad_weight[:, c] = weight
        grad_rotation[:, c] = turn - weight - b0 * ref[0:1, c] - b1 * ref[1:2, c]
    grad_bias[...] = extra[4, 0:4]
    for copy in sends:
        copy.wait()


def call(kernel, specs, outs, scratch=(), far_outs=(), mib=8, flops=1e8, bytes_accessed=2e6):
    return pl.pallas_call(
        kernel,
        in_specs=[{"s": SMEM, "v": VMEM, "a": ANY}[s] for s in specs],
        out_specs=[ANY if n in far_outs else VMEM for n in range(len(outs))],
        out_shape=[jax.ShapeDtypeStruct(s, d) for s, d in outs],
        scratch_shapes=scratch,
        compiler_params=pltpu.CompilerParams(vmem_limit_bytes=mib * 1024 * 1024),
        cost_estimate=pl.CostEstimate(
            flops=int(flops), bytes_accessed=int(bytes_accessed), transcendentals=0
        ),
    )


def swap(x, axes):
    return lax.all_to_all(x, axes, 0, 0, tiled=False)


def ahead(x, d):
    return lax.ppermute(x, "zh", [(i, i + d) for i in range(4 - d)])


def shards(queries, key_rows, values, out_grad, rate, rotation, refusal, proj_weight, proj_bias, positions):
    q, k, v, grad = queries[0], key_rows[0], values[0], out_grad[0]
    ref = refusal.T
    bias = jnp.pad(proj_bias, (0, 124))[None, :]
    rows = (BLOCK, WIDE)
    tile = (NPOS, 128)

    def space(shape, dtype=f32):
        return pltpu.VMEM(shape, dtype)

    def marks(*shape):
        return pltpu.SemaphoreType.DMA(shape)

    grad_state, small, logs, places = call(
        query_state,
        "ssaaaavvv",
        [((16, 96, 128), f32), ((24, 128), f32), ((8, 128), f32), (tile, jnp.int32)],
        [space(rows, bf16)] * 4 + [space((16, 96, 128)), marks(4), marks(2 * HEADS)],
        (0,),
        mib=60,
    )(rate, positions, q, k, grad, v, rotation, ref, proj_weight)
    later = swap(grad_state, NEAR)
    small = lax.psum(small, "head")
    moved, state, basis = call(
        key_state,
        "vvvvvvvvv",
        [(rows, bf16), ((16, 64, 128), f32), ((HEADS, 16, 128), f32)],
        [space((16, 64, 128)), marks(HEADS)],
        (1,),
    )(logs, places, small, v, k, rotation, ref, proj_weight, bias)
    state, later = lax.optimization_barrier((state, later))
    earlier = swap(state, NEAR)
    (own,) = call(backward_totals, "vv", [((96, 128), f32)], [space(tile)])(logs, later)
    groups = lax.all_gather(own, "zh")
    groups, earlier = lax.optimization_barrier((groups, earlier))
    (total,) = call(forward_totals, "vv", [((64, 128), f32)])(logs, earlier)
    passed = [ahead(total, d) for d in (2, 1, 3)]
    one, two, three = passed[1], passed[0], passed[2]
    (leaving,) = call(
        backward_carried,
        "vvvv",
        [((16, 88, 128), f32)],
        [space((16, 88, 128)), space(tile), marks(4)],
        (0,),
    )(logs, later, groups, basis)
    leaving, total = lax.optimization_barrier((leaving, total))
    leaving = swap(leaving, NEAR)
    (entering,) = call(
        forward_carried,
        "vvvvv",
        [((16, 64, 128), f32)],
        [space((16, 64, 128)), marks(4)],
        (0,),
    )(logs, earlier, one, two, three)
    (head_sums,) = call(sum_slices, "v", [(tile, f32)])(leaving)
    head_sums = lax.psum(head_sums, "head")
    entering = swap(entering, NEAR)
    (parts,) = call(products, "vvv", [((72, 128), f32)])(head_sums, bias, leaving)
    others = lax.ppermute(parts, "dp", [(0, 1), (1, 0)])
    attended_in, grad_q_in, grad_k, grad_v = call(
        backward_rest, "vvvvvvvvv", [(rows, f32)] * 2 + [(rows, bf16)] * 2
    )(logs, places, q, k, moved, grad, leaving, basis, head_sums)
    attended, grad_q, grad_rotation, grad_weight, grad_bias = call(
        forward_rest,
        "vvvvvvvvvv",
        [(rows, bf16)] * 2 + [((4, WIDE), f32)] * 2 + [((4,), f32)],
        [space(rows, bf16)] * 2 + [marks(4, 2)],
        (0, 1),
    )(logs, q, grad, entering, attended_in, grad_q_in, small, ref, parts, others)
    return (
        attended[None],
        grad_q[None],
        grad_k[None],
        grad_v[None],
        grad_rotation,
        grad_weight,
        grad_bias,
    )


def solution(mesh):
    own = Mesh(mesh.devices.reshape(4, 4, 4, 4, 2), ("zh", "zl", "y", "head", "dp"))
    seq = ("zh", "zl", "y")
    stream = P("dp", seq, "head")
    return jax.shard_map(
        shards,
        mesh=own,
        in_specs=(
            stream,
            stream,
            stream,
            stream,
            P("head"),
            P(None, "head"),
            P("head", None),
            P(None, "head"),
            P(),
            P("dp", None),
        ),
        out_specs=(stream, stream, stream, stream, P(None, "head"), P(None, "head"), P()),
        check_vma=False,
    )
```

```python
import functools
import jax
import jax.numpy as jnp
from jax import lax
from jax.experimental import pallas as pl
from jax.experimental.pallas import tpu as pltpu
from jax.sharding import Mesh, PartitionSpec as P

highest = lax.Precision.HIGHEST
f32, bf16 = jnp.float32, jnp.bfloat16
BLOCK = 128
HEADS = 8
SIZE = 128
WIDE = HEADS * SIZE
NPOS = 16
NEAR = ("zl", "y")
ANY = pl.BlockSpec(memory_space=pltpu.HBM)
SMEM = pl.BlockSpec(memory_space=pltpu.SMEM)
VMEM = pl.BlockSpec(memory_space=pltpu.VMEM)


def nn(a, b):
    return lax.dot_general(a, b, (((1,), (0,)), ((), ())), preferred_element_type=f32)


def nt(a, b):
    return lax.dot_general(a, b, (((1,), (1,)), ((), ())), preferred_element_type=f32)


def tn(a, b):
    return lax.dot_general(a, b, (((0,), (0,)), ((), ())), preferred_element_type=f32)


def full_nt(a, b):
    return lax.dot_general(
        a, b, (((1,), (1,)), ((), ())), preferred_element_type=f32, precision=highest
    )


def full_tn(a, b):
    return lax.dot_general(
        a, b, (((0,), (0,)), ((), ())), preferred_element_type=f32, precision=highest
    )


def split(x):
    high = x.astype(bf16)
    return high, (x - high.astype(f32)).astype(bf16)


def log_keep(rate):
    total = jnp.float32(1.0 / 8.0)
    for n in range(7, 0, -1):
        total = total * rate + jnp.float32(1.0 / n)
    return -rate * total


def powers(logs, head, exponents):
    return jnp.exp(exponents * logs[pl.ds(head, 1), :])


def rows_iota(shape=(BLOCK, SIZE)):
    return lax.broadcasted_iota(jnp.int32, shape, 0)


def cols_iota(shape=(BLOCK, SIZE)):
    return lax.broadcasted_iota(jnp.int32, shape, 1)


def far_place():
    return lax.axis_index("zh")


def near_place():
    return lax.axis_index("zl") * 4 + lax.axis_index("y")


def block_start():
    return (far_place() * 16 + near_place()) * BLOCK


def local_places(positions, start):
    row = rows_iota((NPOS, BLOCK))
    wanted = jnp.full((NPOS, BLOCK), -1, jnp.int32)
    for j in range(NPOS):
        wanted = jnp.where(row == j, positions[0, j], wanted)
    return wanted - start


def selector(places):
    return (places[...] == cols_iota((NPOS, BLOCK))).astype(bf16)


def head_cols(h):
    return slice(h * SIZE, (h + 1) * SIZE)


def decayed_state(weighted, other):
    high, low = split(weighted)
    both = tn(other, jnp.concatenate([high, low], axis=1))
    return both[:, 0:SIZE] + both[:, SIZE:]


def nn_terms(a, terms):
    return nn(jnp.concatenate([a, a], axis=1), jnp.concatenate(terms, axis=0))


def nt_terms(a, terms):
    return nt(jnp.concatenate([a, a], axis=1), jnp.concatenate(terms, axis=1))


def halves(left, right, odd):
    lane = cols_iota(left.shape)
    if odd:
        return jnp.where(lane < 64, pltpu.roll(left, 64, 1), right)
    return jnp.where(lane < 64, left, pltpu.roll(right, 64, 1))


def query_state(
    rate, positions, q_far, k_far, grad_far, v_far, rot, ref, proj,
    out_far, small, logs, places_out, q, k, grad, v, out, arrived, sent,
):
    fetches = []
    for n, (src, dst) in enumerate(((q_far, q), (grad_far, grad), (k_far, k), (v_far, v))):
        fetch = pltpu.make_async_copy(src, dst, arrived.at[n])
        fetch.start()
        fetches.append(fetch)
    sends = []

    def send(h, start, rows):
        here = (pl.ds(2 * h, 2), pl.ds(start, rows))
        copy = pltpu.make_async_copy(out.at[here], out_far.at[here], sent.at[len(sends)])
        copy.start()
        sends.append(copy)

    for h in range(HEADS):
        logs[h : h + 1, :] = jnp.full((1, 128), log_keep(rate[h]), f32)
    places = local_places(positions, block_start())
    places_out[...] = places
    lane = cols_iota((NPOS, BLOCK))
    select = (places == lane).astype(bf16)
    after = lane - places
    reached = after >= 0
    distance = jnp.maximum(after, 0).astype(f32)
    leave = jnp.clip(BLOCK - places, 0, BLOCK).astype(f32)
    tables = [jnp.where(reached, powers(logs, h, distance), 0.0) for h in range(HEADS)]
    offset = rows_iota().astype(f32)
    for fetch in fetches[:2]:
        fetch.wait()
    for h in range(HEADS):
        c = head_cols(h)
        weighted = q[:, c].astype(f32) * powers(logs, h, offset)
        state = decayed_state(weighted, grad[:, c])
        out[2 * h, 0:64] = state[:64]
        out[2 * h + 1, 0:64] = state[64:]
        send(h, 0, 64)
    for fetch in fetches[2:]:
        fetch.wait()
    keys = nn(select, k[...])
    chosen = nn(select, v[...])
    low = keys.astype(bf16)
    scores = [nt(low[:, head_cols(h)], q[:, head_cols(h)]) for h in range(HEADS)]
    mixing = [(scores[h] * tables[h]).astype(bf16) for h in range(HEADS)]
    local = [nn(mixing[h], grad[:, head_cols(h)]) for h in range(HEADS)]
    for h in range(HEADS):
        c = head_cols(h)
        key = keys[:, c] * powers(logs, h, leave)
        for odd in range(2):
            i = 2 * h + odd
            out[i, 64:80] = key
            out[i, 80:96] = halves(local[h], chosen[:, c], odd)
        send(h, 64, 32)
    left = jnp.concatenate([chosen, ref[...], rot[...], jnp.zeros((2, WIDE), f32)], axis=0)
    right = jnp.concatenate(
        [proj[...] - rot[...], ref[...], rot[...], jnp.zeros((6, WIDE), f32)], axis=0
    )
    small[...] = jnp.zeros((24, 128), f32)
    small[:, 0:16] = full_nt(left, right)
    for copy in sends:
        copy.wait()


def inverse_of(small):
    g00, g01 = small[16:17, 4:5], small[16:17, 5:6]
    g10, g11 = small[17:18, 4:5], small[17:18, 5:6]
    det = g00 * g11 - g01 * g10
    return g11 / det, -g01 / det, -g10 / det, g00 / det


def third_terms(x):
    high = x.astype(bf16)
    rest = x - high.astype(f32)
    middle = rest.astype(bf16)
    low = (rest - middle.astype(f32)).astype(bf16)
    return jnp.concatenate([high, middle, low], axis=0)


def key_state(
    logs, places, small, v, k, rot, ref, proj, bias, moved, state_far, basis, state, sent
):
    i00, i01, i10, i11 = inverse_of(small)
    c0, c1 = small[18:22, 4:5], small[18:22, 5:6]
    rotated = (
        rot[...]
        - (c0 * i00 + c1 * i10) * ref[0:1, :]
        - (c0 * i01 + c1 * i11) * ref[1:2, :]
    )
    lift = proj[...] - rotated
    rows = jnp.concatenate(
        [rotated, ref[...], lift, ref[...], jnp.zeros((4, WIDE), f32)], axis=0
    )
    turned = pltpu.roll(small[16:24, :], 122, 1)
    t0, t1 = turned[0:1], turned[1:2]
    full = (
        small[0:16, :]
        + bias[...]
        + small[0:16, 4:5] * (t0 * i00 + t1 * i10)
        + small[0:16, 5:6] * (t0 * i01 + t1 * i11)
    )
    full = jnp.where(cols_iota((NPOS, 128)) < 4, full, 0.0)
    shift = jnp.zeros((NPOS, WIDE), f32)
    for r in range(4):
        shift = shift + full[:, r : r + 1] * rotated[r : r + 1, :]
    select = selector(places)
    select = jnp.concatenate([select, select, select], axis=0)
    shift = third_terms(shift)
    offset = rows_iota().astype(f32)
    sends = []
    for h in range(HEADS):
        c = head_cols(h)
        basis[h] = rows[:, c]
        new = (v[:, c].astype(f32) + tn(select, shift[:, c])).astype(bf16)
        moved[:, c] = new
        weighted = k[:, c].astype(f32) * powers(logs, h, BLOCK - 1.0 - offset)
        out = decayed_state(weighted, new)
        state[2 * h] = out[:64]
        state[2 * h + 1] = out[64:]
        part = pl.ds(2 * h, 2)
        send = pltpu.make_async_copy(state.at[part], state_far.at[part], sent.at[h])
        send.start()
        sends.append(send)
    for send in sends:
        send.wait()


def dot3(a, b):
    ah, al = split(a)
    bh, bl = split(b)
    return nt(ah, bh) + (nt(al, bh) + nt(ah, bl))


def backward_totals(logs, later, out, gathered):
    keep = powers(logs, near_place() // 2, jnp.full((64, 128), float(BLOCK), f32))
    keep_key = keep[0:NPOS]
    state = later[15, 0:64]
    key = later[0, 64:80]
    rows = later[15, 80:96]
    gathered[...] = jnp.zeros((NPOS, 128), f32)
    for b in range(14, -1, -1):
        gathered[:, 0:64] += dot3(later[b, 64:80], state)
        rows = rows + later[b, 80:96]
        state = state * keep + later[b, 0:64]
    for b in range(1, 16):
        key = key * keep_key + later[b, 64:80]
    out[0:64] = state
    out[64:80] = key
    out[80:96] = rows + gathered[...]


def backward_carried(
    logs, later, groups, basis, out_far, out, gathered, sent
):
    far, near = far_place(), near_place()
    exponent = jnp.full((64, 128), float(BLOCK), f32)
    keep = powers(logs, near // 2, exponent)
    keep_group = powers(logs, near // 2, exponent * 16.0)
    rows = groups[3, 80:96]
    gathered[...] = jnp.zeros((NPOS, 128), f32)
    carry = jnp.zeros((64, 128), f32)
    state = carry
    for z in (2, 1, 0):
        carry = carry * keep_group + groups[z + 1, 0:64]
        gathered[:, 0:64] += dot3(groups[z, 64:80], carry)
        rows = rows + groups[z, 80:96]
        state = jnp.where(far == z, carry, state)
    rows = rows + gathered[...]
    both = basis[near // 2]
    turned = pltpu.roll(both, 64, 1)
    odd = near % 2 == 1
    lane, row = cols_iota((16, 128)), rows_iota((16, 128))
    for_grad = jnp.where(odd, turned, both)
    for_value = jnp.where(odd, both, turned)
    right = jnp.where(
        row < 6,
        jnp.where(lane < 64, for_grad, 0.0),
        jnp.where(lane < 64, 0.0, for_value),
    )
    gathered[...] = jnp.zeros((NPOS, 128), f32)
    gathered[:, 0:16] = full_nt(rows, right)
    packed = gathered[0:8] + pltpu.roll(gathered[8:16], 16, 1)
    sends = []
    for b in range(15, -1, -1):
        out[b, 0:64] = state
        out[b, 64:72] = packed
        out[b, 72:88] = rows
        state = state * keep + later[b, 0:64]
        if b % 4 == 0:
            part = pl.ds(b, 4)
            send = pltpu.make_async_copy(out.at[part], out_far.at[part], sent.at[b // 4])
            send.start()
            sends.append(send)
    for send in sends:
        send.wait()


def forward_totals(logs, earlier, out):
    keep = powers(logs, near_place() // 2, jnp.full((64, 128), float(BLOCK), f32))
    state = earlier[0]
    for b in range(1, 16):
        state = state * keep + earlier[b]
    out[...] = state


def forward_carried(logs, earlier, one, two, three, out_far, out, sent):
    exponent = jnp.full((64, 128), float(BLOCK), f32)
    keep = powers(logs, near_place() // 2, exponent)
    keep_group = powers(logs, near_place() // 2, exponent * 16.0)
    state = (three[...] * keep_group + two[...]) * keep_group + one[...]
    sends = []
    for b in range(16):
        out[b] = state
        state = state * keep + earlier[b]
        if b % 4 == 3:
            part = pl.ds(b - 3, 4)
            send = pltpu.make_async_copy(out.at[part], out_far.at[part], sent.at[b // 4])
            send.start()
            sends.append(send)
    for send in sends:
        send.wait()


def sum_slices(x, out):
    total = x[0, 64:72]
    for i in range(1, 16):
        total = total + x[i, 64:72]
    lane = cols_iota((8, 128))
    out[0:8] = jnp.where(lane < 16, total, 0.0)
    out[8:16] = jnp.where(lane < 16, pltpu.roll(total, 112, 1), 0.0)


def products(head_sums, bias, x, parts):
    lane = cols_iota((NPOS, 128))
    sums = head_sums[...]
    turned = pltpu.roll(sums, 122, 1)
    code_grad = jnp.where(lane < 4, sums, 0.0)
    code = jnp.where(lane < 4, turned + bias[...], 0.0)
    both = code_grad + pltpu.roll(code, 4, 1)
    lane = cols_iota((4, 128))
    wide = jnp.concatenate([x[i, 72:88] for i in range(16)], axis=1)
    every = lax.dot_general(
        jnp.transpose(both)[0:8],
        wide,
        (((1,), (0,)), ((), ())),
        preferred_element_type=f32,
        precision=highest,
    )
    for i in range(16):
        got = every[:, head_cols(i)]
        parts[4 * i : 4 * i + 4] = jnp.where(lane < 64, got[4:8], got[0:4])
    along = (full_tn(code, sums) - full_tn(code_grad, turned))[0:4]
    total = jnp.broadcast_to(jnp.sum(code_grad, axis=0, keepdims=True), (4, 128))
    parts[64:68] = along
    parts[68:72] = total


def backward_rest(
    logs, places, q, k, moved, grad, state, basis, head_sums, attended, grad_q,
    grad_k_far, grad_v_far, grad_k, grad_v, sent,
):
    sends = []
    between = rows_iota() - cols_iota()
    lower = between >= 0
    distance = jnp.maximum(between, 0).astype(f32)
    offset = rows_iota().astype(f32)
    select = selector(places)
    select = jnp.concatenate([select, select, select], axis=0)
    code_grad = head_sums[...]
    for h in range(HEADS):
        c = head_cols(h)
        table = jnp.where(lower, powers(logs, h, distance), 0.0)
        leave = powers(logs, h, BLOCK - offset)
        terms = split(jnp.concatenate([state[2 * h, 0:64], state[2 * h + 1, 0:64]], axis=0))
        qh, mh, kh, gh = q[:, c], moved[:, c], k[:, c], grad[:, c]
        mixing = (nt(qh, kh) * table).astype(bf16)
        grad_mixing = (nt(gh, mh) * table).astype(bf16)
        attended[:, c] = nn(mixing, mh)
        grad_q[:, c] = nn(grad_mixing, kh)
        inner = tn(grad_mixing, qh)
        grad_k[:, c] = (inner + leave * nn_terms(mh, terms)).astype(bf16)
        inner = tn(mixing, gh)
        lift = basis[h][6:10]
        fix = jnp.zeros((NPOS, SIZE), f32)
        for r in range(4):
            fix = fix + code_grad[:, r : r + 1] * lift[r : r + 1]
        out = inner + leave * nt_terms(kh, terms)
        grad_v[:, c] = (out + tn(select, third_terms(fix))).astype(bf16)
        if h % 2 == 1:
            wide = slice((h - 1) * SIZE, (h + 1) * SIZE)
            for n, (src, dst) in enumerate(((grad_k, grad_k_far), (grad_v, grad_v_far))):
                copy = pltpu.make_async_copy(src.at[:, wide], dst.at[:, wide], sent.at[h // 2, n])
                copy.start()
                sends.append(copy)
    for copy in sends:
        copy.wait()


def forward_rest(
    logs, q, grad, state, attended_in, grad_q_in, small, ref, parts, others,
    attended_far, grad_q_far, grad_rotation, grad_weight, grad_bias, attended, grad_q, sent,
):
    sends = []
    offset = rows_iota().astype(f32)
    i00, i01, i10, i11 = inverse_of(small)
    extra = parts[64:72] + others[64:72]
    a0, a1 = extra[0:4, 4:5], extra[0:4, 5:6]
    b0 = a0 * i00 + a1 * i10
    b1 = a0 * i01 + a1 * i11
    lane = cols_iota((4, 128))
    for h in range(HEADS):
        c = head_cols(h)
        enter = powers(logs, h, offset + 1.0)
        terms = split(jnp.concatenate([state[2 * h], state[2 * h + 1]], axis=0))
        qh, gh = q[:, c], grad[:, c]
        attended[:, c] = (attended_in[:, c] + enter * nt_terms(qh, terms)).astype(bf16)
        grad_q[:, c] = (grad_q_in[:, c] + enter * nn_terms(gh, terms)).astype(bf16)
        if h % 2 == 1:
            wide = slice((h - 1) * SIZE, (h + 1) * SIZE)
            pairs = ((attended, attended_far), (grad_q, grad_q_far))
            for n, (src, dst) in enumerate(pairs):
                copy = pltpu.make_async_copy(src.at[:, wide], dst.at[:, wide], sent.at[h // 2, n])
                copy.start()
                sends.append(copy)
        both = parts[8 * h : 8 * h + 8] + others[8 * h : 8 * h + 8]
        turned = pltpu.roll(both, 64, 1)
        turn = jnp.where(lane < 64, both[0:4], turned[4:8])
        weight = jnp.where(lane < 64, turned[0:4], both[4:8])
        grad_weight[:, c] = weight
        grad_rotation[:, c] = turn - weight - b0 * ref[0:1, c] - b1 * ref[1:2, c]
    grad_bias[...] = extra[4, 0:4]
    for copy in sends:
        copy.wait()


def call(kernel, specs, outs, scratch=(), far_outs=(), mib=8, flops=1e8, bytes_accessed=2e6):
    return pl.pallas_call(
        kernel,
        in_specs=[{"s": SMEM, "v": VMEM, "a": ANY}[s] for s in specs],
        out_specs=[ANY if n in far_outs else VMEM for n in range(len(outs))],
        out_shape=[jax.ShapeDtypeStruct(s, d) for s, d in outs],
        scratch_shapes=scratch,
        compiler_params=pltpu.CompilerParams(vmem_limit_bytes=mib * 1024 * 1024),
        cost_estimate=pl.CostEstimate(
            flops=int(flops), bytes_accessed=int(bytes_accessed), transcendentals=0
        ),
    )


def swap(x, axes):
    return lax.all_to_all(x, axes, 0, 0, tiled=False)


def ahead(x, d):
    return lax.ppermute(x, "zh", [(i, i + d) for i in range(4 - d)])


def shards(queries, key_rows, values, out_grad, rate, rotation, refusal, proj_weight, proj_bias, positions):
    q, k, v, grad = queries[0], key_rows[0], values[0], out_grad[0]
    ref = refusal.T
    bias = jnp.pad(proj_bias, (0, 124))[None, :]
    rows = (BLOCK, WIDE)
    tile = (NPOS, 128)

    def space(shape, dtype=f32):
        return pltpu.VMEM(shape, dtype)

    def marks(*shape):
        return pltpu.SemaphoreType.DMA(shape)

    grad_state, small, logs, places = call(
        query_state,
        "ssaaaavvv",
        [((16, 96, 128), f32), ((24, 128), f32), ((8, 128), f32), (tile, jnp.int32)],
        [space(rows, bf16)] * 4 + [space((16, 96, 128)), marks(4), marks(2 * HEADS)],
        (0,),
        mib=60,
    )(rate, positions, q, k, grad, v, rotation, ref, proj_weight)
    later = swap(grad_state, NEAR)
    small = lax.psum(small, "head")
    moved, state, basis = call(
        key_state,
        "vvvvvvvvv",
        [(rows, bf16), ((16, 64, 128), f32), ((HEADS, 16, 128), f32)],
        [space((16, 64, 128)), marks(HEADS)],
        (1,),
    )(logs, places, small, v, k, rotation, ref, proj_weight, bias)
    state, later = lax.optimization_barrier((state, later))
    earlier = swap(state, NEAR)
    (own,) = call(backward_totals, "vv", [((96, 128), f32)], [space(tile)])(logs, later)
    groups = lax.all_gather(own, "zh")
    groups, earlier = lax.optimization_barrier((groups, earlier))
    (total,) = call(forward_totals, "vv", [((64, 128), f32)])(logs, earlier)
    passed = [ahead(total, d) for d in (2, 1, 3)]
    one, two, three = passed[1], passed[0], passed[2]
    (leaving,) = call(
        backward_carried,
        "vvvv",
        [((16, 88, 128), f32)],
        [space((16, 88, 128)), space(tile), marks(4)],
        (0,),
    )(logs, later, groups, basis)
    leaving, total = lax.optimization_barrier((leaving, total))
    leaving = swap(leaving, NEAR)
    (entering,) = call(
        forward_carried,
        "vvvvv",
        [((16, 64, 128), f32)],
        [space((16, 64, 128)), marks(4)],
        (0,),
    )(logs, earlier, one, two, three)
    (head_sums,) = call(sum_slices, "v", [(tile, f32)])(leaving)
    head_sums = lax.psum(head_sums, "head")
    entering = swap(entering, NEAR)
    (parts,) = call(products, "vvv", [((72, 128), f32)])(head_sums, bias, leaving)
    others = lax.ppermute(parts, "dp", [(0, 1), (1, 0)])
    attended_in, grad_q_in, grad_k, grad_v = call(
        backward_rest,
        "v" * 9,
        [(rows, f32)] * 2 + [(rows, bf16)] * 2,
        [space(rows, bf16)] * 2 + [marks(4, 2)],
        (2, 3),
    )(logs, places, q, k, moved, grad, leaving, basis, head_sums)
    attended, grad_q, grad_rotation, grad_weight, grad_bias = call(
        forward_rest,
        "vvvvvvvvvv",
        [(rows, bf16)] * 2 + [((4, WIDE), f32)] * 2 + [((4,), f32)],
        [space(rows, bf16)] * 2 + [marks(4, 2)],
        (0, 1),
    )(logs, q, grad, entering, attended_in, grad_q_in, small, ref, parts, others)
    return (
        attended[None],
        grad_q[None],
        grad_k[None],
        grad_v[None],
        grad_rotation,
        grad_weight,
        grad_bias,
    )


def solution(mesh):
    own = Mesh(mesh.devices.reshape(4, 4, 4, 4, 2), ("zh", "zl", "y", "head", "dp"))
    seq = ("zh", "zl", "y")
    stream = P("dp", seq, "head")
    return jax.shard_map(
        shards,
        mesh=own,
        in_specs=(
            stream,
            stream,
            stream,
            stream,
            P("head"),
            P(None, "head"),
            P("head", None),
            P(None, "head"),
            P(),
            P("dp", None),
        ),
        out_specs=(stream, stream, stream, stream, P(None, "head"), P(None, "head"), P()),
        check_vma=False,
    )
```

```python
import functools
import jax
import jax.numpy as jnp
from jax import lax
from jax.experimental import pallas as pl
from jax.experimental.pallas import tpu as pltpu
from jax.sharding import Mesh, PartitionSpec as P

highest = lax.Precision.HIGHEST
f32, bf16 = jnp.float32, jnp.bfloat16
BLOCK = 128
HEADS = 8
SIZE = 128
WIDE = HEADS * SIZE
NPOS = 16
NEAR = ("zl", "y")
ANY = pl.BlockSpec(memory_space=pltpu.HBM)
SMEM = pl.BlockSpec(memory_space=pltpu.SMEM)
VMEM = pl.BlockSpec(memory_space=pltpu.VMEM)


def nn(a, b):
    return lax.dot_general(a, b, (((1,), (0,)), ((), ())), preferred_element_type=f32)


def nt(a, b):
    return lax.dot_general(a, b, (((1,), (1,)), ((), ())), preferred_element_type=f32)


def tn(a, b):
    return lax.dot_general(a, b, (((0,), (0,)), ((), ())), preferred_element_type=f32)


def full_nt(a, b):
    return lax.dot_general(
        a, b, (((1,), (1,)), ((), ())), preferred_element_type=f32, precision=highest
    )


def full_tn(a, b):
    return lax.dot_general(
        a, b, (((0,), (0,)), ((), ())), preferred_element_type=f32, precision=highest
    )


def split(x):
    high = x.astype(bf16)
    return high, (x - high.astype(f32)).astype(bf16)


def log_keep(rate):
    total = jnp.float32(1.0 / 8.0)
    for n in range(7, 0, -1):
        total = total * rate + jnp.float32(1.0 / n)
    return -rate * total


def powers(logs, head, exponents):
    return jnp.exp(exponents * logs[pl.ds(head, 1), :])


def rows_iota(shape=(BLOCK, SIZE)):
    return lax.broadcasted_iota(jnp.int32, shape, 0)


def cols_iota(shape=(BLOCK, SIZE)):
    return lax.broadcasted_iota(jnp.int32, shape, 1)


def far_place():
    return lax.axis_index("zh")


def near_place():
    return lax.axis_index("zl") * 4 + lax.axis_index("y")


def block_start():
    return (far_place() * 16 + near_place()) * BLOCK


def local_places(positions, start):
    row = rows_iota((NPOS, BLOCK))
    wanted = jnp.full((NPOS, BLOCK), -1, jnp.int32)
    for j in range(NPOS):
        wanted = jnp.where(row == j, positions[0, j], wanted)
    return wanted - start


def selector(places):
    return (places[...] == cols_iota((NPOS, BLOCK))).astype(bf16)


def head_cols(h):
    return slice(h * SIZE, (h + 1) * SIZE)


def decayed_state(weighted, other):
    high, low = split(weighted)
    both = tn(other, jnp.concatenate([high, low], axis=1))
    return both[:, 0:SIZE] + both[:, SIZE:]


def nn_terms(a, terms):
    return nn(jnp.concatenate([a, a], axis=1), jnp.concatenate(terms, axis=0))


def nt_terms(a, terms):
    return nt(jnp.concatenate([a, a], axis=1), jnp.concatenate(terms, axis=1))


def halves(left, right, odd):
    lane = cols_iota(left.shape)
    if odd:
        return jnp.where(lane < 64, pltpu.roll(left, 64, 1), right)
    return jnp.where(lane < 64, left, pltpu.roll(right, 64, 1))


def query_state(
    rate, positions, q_far, k_far, grad_far, v_far, rot, ref, proj,
    out_far, small, logs, places_out, q, k, grad, v, out, arrived, sent,
):
    fetches = []
    for n, (src, dst) in enumerate(((q_far, q), (grad_far, grad), (k_far, k), (v_far, v))):
        fetch = pltpu.make_async_copy(src, dst, arrived.at[n])
        fetch.start()
        fetches.append(fetch)
    sends = []

    def send(h, start, rows):
        here = (pl.ds(2 * h, 2), pl.ds(start, rows))
        copy = pltpu.make_async_copy(out.at[here], out_far.at[here], sent.at[len(sends)])
        copy.start()
        sends.append(copy)

    for h in range(HEADS):
        logs[h : h + 1, :] = jnp.full((1, 128), log_keep(rate[h]), f32)
    places = local_places(positions, block_start())
    places_out[...] = places
    lane = cols_iota((NPOS, BLOCK))
    select = (places == lane).astype(bf16)
    after = lane - places
    reached = after >= 0
    distance = jnp.maximum(after, 0).astype(f32)
    leave = jnp.clip(BLOCK - places, 0, BLOCK).astype(f32)
    tables = [jnp.where(reached, powers(logs, h, distance), 0.0) for h in range(HEADS)]
    offset = rows_iota().astype(f32)
    for fetch in fetches[:2]:
        fetch.wait()
    for h in range(HEADS):
        c = head_cols(h)
        weighted = q[:, c].astype(f32) * powers(logs, h, offset)
        state = decayed_state(weighted, grad[:, c])
        out[2 * h, 0:64] = state[:64]
        out[2 * h + 1, 0:64] = state[64:]
        send(h, 0, 64)
    for fetch in fetches[2:]:
        fetch.wait()
    keys = nn(select, k[...])
    chosen = nn(select, v[...])
    low = keys.astype(bf16)
    scores = [nt(low[:, head_cols(h)], q[:, head_cols(h)]) for h in range(HEADS)]
    mixing = [(scores[h] * tables[h]).astype(bf16) for h in range(HEADS)]
    local = [nn(mixing[h], grad[:, head_cols(h)]) for h in range(HEADS)]
    for h in range(HEADS):
        c = head_cols(h)
        key = keys[:, c] * powers(logs, h, leave)
        for odd in range(2):
            i = 2 * h + odd
            out[i, 64:80] = key
            out[i, 80:96] = halves(local[h], chosen[:, c], odd)
        send(h, 64, 32)
    left = jnp.concatenate([chosen, ref[...], rot[...], jnp.zeros((2, WIDE), f32)], axis=0)
    right = jnp.concatenate(
        [proj[...] - rot[...], ref[...], rot[...], jnp.zeros((6, WIDE), f32)], axis=0
    )
    small[...] = jnp.zeros((24, 128), f32)
    small[:, 0:16] = full_nt(left, right)
    for copy in sends:
        copy.wait()


def inverse_of(small):
    g00, g01 = small[16:17, 4:5], small[16:17, 5:6]
    g10, g11 = small[17:18, 4:5], small[17:18, 5:6]
    det = g00 * g11 - g01 * g10
    return g11 / det, -g01 / det, -g10 / det, g00 / det


def third_terms(x):
    high = x.astype(bf16)
    rest = x - high.astype(f32)
    middle = rest.astype(bf16)
    low = (rest - middle.astype(f32)).astype(bf16)
    return jnp.concatenate([high, middle, low], axis=0)


def key_state(
    logs, places, small, v, k, rot, ref, proj, bias, moved, state_far, basis, state, sent
):
    i00, i01, i10, i11 = inverse_of(small)
    c0, c1 = small[18:22, 4:5], small[18:22, 5:6]
    rotated = (
        rot[...]
        - (c0 * i00 + c1 * i10) * ref[0:1, :]
        - (c0 * i01 + c1 * i11) * ref[1:2, :]
    )
    lift = proj[...] - rotated
    rows = jnp.concatenate(
        [rotated, ref[...], lift, ref[...], jnp.zeros((4, WIDE), f32)], axis=0
    )
    turned = pltpu.roll(small[16:24, :], 122, 1)
    t0, t1 = turned[0:1], turned[1:2]
    full = (
        small[0:16, :]
        + bias[...]
        + small[0:16, 4:5] * (t0 * i00 + t1 * i10)
        + small[0:16, 5:6] * (t0 * i01 + t1 * i11)
    )
    full = jnp.where(cols_iota((NPOS, 128)) < 4, full, 0.0)
    shift = jnp.zeros((NPOS, WIDE), f32)
    for r in range(4):
        shift = shift + full[:, r : r + 1] * rotated[r : r + 1, :]
    select = selector(places)
    select = jnp.concatenate([select, select, select], axis=0)
    shift = third_terms(shift)
    offset = rows_iota().astype(f32)
    sends = []
    for h in range(HEADS):
        c = head_cols(h)
        basis[h] = rows[:, c]
        new = (v[:, c].astype(f32) + tn(select, shift[:, c])).astype(bf16)
        moved[:, c] = new
        weighted = k[:, c].astype(f32) * powers(logs, h, BLOCK - 1.0 - offset)
        out = decayed_state(weighted, new)
        state[2 * h] = out[:64]
        state[2 * h + 1] = out[64:]
        part = pl.ds(2 * h, 2)
        send = pltpu.make_async_copy(state.at[part], state_far.at[part], sent.at[h])
        send.start()
        sends.append(send)
    for send in sends:
        send.wait()


def dot3(a, b):
    ah, al = split(a)
    bh, bl = split(b)
    return nt(ah, bh) + (nt(al, bh) + nt(ah, bl))


def backward_totals(logs, later, out, gathered):
    keep = powers(logs, near_place() // 2, jnp.full((64, 128), float(BLOCK), f32))
    keep_key = keep[0:NPOS]
    state = later[15, 0:64]
    key = later[0, 64:80]
    rows = later[15, 80:96]
    gathered[...] = jnp.zeros((NPOS, 128), f32)
    for b in range(14, -1, -1):
        gathered[:, 0:64] += dot3(later[b, 64:80], state)
        rows = rows + later[b, 80:96]
        state = state * keep + later[b, 0:64]
    for b in range(1, 16):
        key = key * keep_key + later[b, 64:80]
    out[0:64] = state
    out[64:80] = key
    out[80:96] = rows + gathered[...]


def backward_carried(
    logs, later, groups, basis, out_far, out, gathered, sent
):
    far, near = far_place(), near_place()
    exponent = jnp.full((64, 128), float(BLOCK), f32)
    keep = powers(logs, near // 2, exponent)
    keep_group = powers(logs, near // 2, exponent * 16.0)
    rows = groups[3, 80:96]
    gathered[...] = jnp.zeros((NPOS, 128), f32)
    carry = jnp.zeros((64, 128), f32)
    state = carry
    for z in (2, 1, 0):
        carry = carry * keep_group + groups[z + 1, 0:64]
        gathered[:, 0:64] += dot3(groups[z, 64:80], carry)
        rows = rows + groups[z, 80:96]
        state = jnp.where(far == z, carry, state)
    rows = rows + gathered[...]
    both = basis[near // 2]
    turned = pltpu.roll(both, 64, 1)
    odd = near % 2 == 1
    lane, row = cols_iota((16, 128)), rows_iota((16, 128))
    for_grad = jnp.where(odd, turned, both)
    for_value = jnp.where(odd, both, turned)
    right = jnp.where(
        row < 6,
        jnp.where(lane < 64, for_grad, 0.0),
        jnp.where(lane < 64, 0.0, for_value),
    )
    gathered[...] = jnp.zeros((NPOS, 128), f32)
    gathered[:, 0:16] = full_nt(rows, right)
    packed = gathered[0:8] + pltpu.roll(gathered[8:16], 16, 1)
    sends = []
    for b in range(15, -1, -1):
        out[b, 0:64] = state
        out[b, 64:72] = packed
        out[b, 72:88] = rows
        state = state * keep + later[b, 0:64]
        if b % 4 == 0:
            part = pl.ds(b, 4)
            send = pltpu.make_async_copy(out.at[part], out_far.at[part], sent.at[b // 4])
            send.start()
            sends.append(send)
    for send in sends:
        send.wait()


def forward_totals(logs, earlier, out):
    keep = powers(logs, near_place() // 2, jnp.full((64, 128), float(BLOCK), f32))
    state = earlier[0]
    for b in range(1, 16):
        state = state * keep + earlier[b]
    out[...] = state


def forward_carried(logs, earlier, one, two, three, out_far, out, sent):
    exponent = jnp.full((64, 128), float(BLOCK), f32)
    keep = powers(logs, near_place() // 2, exponent)
    keep_group = powers(logs, near_place() // 2, exponent * 16.0)
    state = (three[...] * keep_group + two[...]) * keep_group + one[...]
    sends = []
    for b in range(16):
        out[b] = state
        state = state * keep + earlier[b]
        if b % 4 == 3:
            part = pl.ds(b - 3, 4)
            send = pltpu.make_async_copy(out.at[part], out_far.at[part], sent.at[b // 4])
            send.start()
            sends.append(send)
    for send in sends:
        send.wait()


def sum_slices(x, out):
    total = x[0, 64:72]
    for i in range(1, 16):
        total = total + x[i, 64:72]
    lane = cols_iota((8, 128))
    out[0:8] = jnp.where(lane < 16, total, 0.0)
    out[8:16] = jnp.where(lane < 16, pltpu.roll(total, 112, 1), 0.0)


def products(head_sums, bias, x, parts):
    lane = cols_iota((NPOS, 128))
    sums = head_sums[...]
    turned = pltpu.roll(sums, 122, 1)
    code_grad = jnp.where(lane < 4, sums, 0.0)
    code = jnp.where(lane < 4, turned + bias[...], 0.0)
    both = code_grad + pltpu.roll(code, 4, 1)
    lane = cols_iota((4, 128))
    wide = jnp.concatenate([x[i, 72:88] for i in range(16)], axis=1)
    every = lax.dot_general(
        jnp.transpose(both)[0:8],
        wide,
        (((1,), (0,)), ((), ())),
        preferred_element_type=f32,
        precision=highest,
    )
    for i in range(16):
        got = every[:, head_cols(i)]
        parts[4 * i : 4 * i + 4] = jnp.where(lane < 64, got[4:8], got[0:4])
    along = (full_tn(code, sums) - full_tn(code_grad, turned))[0:4]
    total = jnp.broadcast_to(jnp.sum(code_grad, axis=0, keepdims=True), (4, 128))
    parts[64:68] = along
    parts[68:72] = total


def backward_rest(
    logs, places, q, k, moved, grad, state, basis, head_sums, attended, grad_q,
    grad_k_far, grad_v_far, grad_k, grad_v, sent,
):
    sends = []
    between = rows_iota() - cols_iota()
    lower = between >= 0
    distance = jnp.maximum(between, 0).astype(f32)
    offset = rows_iota().astype(f32)
    select = selector(places)
    select = jnp.concatenate([select, select, select], axis=0)
    code_grad = head_sums[...]
    lift = jnp.concatenate([basis[h][6:10] for h in range(HEADS)], axis=1)
    fix = jnp.zeros((NPOS, WIDE), f32)
    for r in range(4):
        fix = fix + code_grad[:, r : r + 1] * lift[r : r + 1]
    fix = tn(select, third_terms(fix))
    for h in range(HEADS):
        c = head_cols(h)
        table = jnp.where(lower, powers(logs, h, distance), 0.0)
        leave = powers(logs, h, BLOCK - offset)
        terms = split(jnp.concatenate([state[2 * h, 0:64], state[2 * h + 1, 0:64]], axis=0))
        qh, mh, kh, gh = q[:, c], moved[:, c], k[:, c], grad[:, c]
        mixing = (nt(qh, kh) * table).astype(bf16)
        grad_mixing = (nt(gh, mh) * table).astype(bf16)
        attended[:, c] = nn(mixing, mh)
        grad_q[:, c] = nn(grad_mixing, kh)
        inner = tn(grad_mixing, qh)
        grad_k[:, c] = (inner + leave * nn_terms(mh, terms)).astype(bf16)
        inner = tn(mixing, gh)
        out = inner + leave * nt_terms(kh, terms)
        grad_v[:, c] = (out + fix[:, c]).astype(bf16)
        if h % 2 == 1:
            wide = slice((h - 1) * SIZE, (h + 1) * SIZE)
            for n, (src, dst) in enumerate(((grad_k, grad_k_far), (grad_v, grad_v_far))):
                copy = pltpu.make_async_copy(src.at[:, wide], dst.at[:, wide], sent.at[h // 2, n])
                copy.start()
                sends.append(copy)
    for copy in sends:
        copy.wait()


def forward_rest(
    logs, q, grad, state, attended_in, grad_q_in, small, ref, parts, others,
    attended_far, grad_q_far, grad_rotation, grad_weight, grad_bias, attended, grad_q, sent,
):
    sends = []
    offset = rows_iota().astype(f32)
    i00, i01, i10, i11 = inverse_of(small)
    extra = parts[64:72] + others[64:72]
    a0, a1 = extra[0:4, 4:5], extra[0:4, 5:6]
    b0 = a0 * i00 + a1 * i10
    b1 = a0 * i01 + a1 * i11
    lane = cols_iota((4, 128))
    for h in range(HEADS):
        c = head_cols(h)
        enter = powers(logs, h, offset + 1.0)
        terms = split(jnp.concatenate([state[2 * h], state[2 * h + 1]], axis=0))
        qh, gh = q[:, c], grad[:, c]
        attended[:, c] = (attended_in[:, c] + enter * nt_terms(qh, terms)).astype(bf16)
        grad_q[:, c] = (grad_q_in[:, c] + enter * nn_terms(gh, terms)).astype(bf16)
        if h % 2 == 1:
            wide = slice((h - 1) * SIZE, (h + 1) * SIZE)
            pairs = ((attended, attended_far), (grad_q, grad_q_far))
            for n, (src, dst) in enumerate(pairs):
                copy = pltpu.make_async_copy(src.at[:, wide], dst.at[:, wide], sent.at[h // 2, n])
                copy.start()
                sends.append(copy)
        both = parts[8 * h : 8 * h + 8] + others[8 * h : 8 * h + 8]
        turned = pltpu.roll(both, 64, 1)
        turn = jnp.where(lane < 64, both[0:4], turned[4:8])
        weight = jnp.where(lane < 64, turned[0:4], both[4:8])
        grad_weight[:, c] = weight
        grad_rotation[:, c] = turn - weight - b0 * ref[0:1, c] - b1 * ref[1:2, c]
    grad_bias[...] = extra[4, 0:4]
    for copy in sends:
        copy.wait()


def call(kernel, specs, outs, scratch=(), far_outs=(), mib=8, flops=1e8, bytes_accessed=2e6):
    return pl.pallas_call(
        kernel,
        in_specs=[{"s": SMEM, "v": VMEM, "a": ANY}[s] for s in specs],
        out_specs=[ANY if n in far_outs else VMEM for n in range(len(outs))],
        out_shape=[jax.ShapeDtypeStruct(s, d) for s, d in outs],
        scratch_shapes=scratch,
        compiler_params=pltpu.CompilerParams(vmem_limit_bytes=mib * 1024 * 1024),
        cost_estimate=pl.CostEstimate(
            flops=int(flops), bytes_accessed=int(bytes_accessed), transcendentals=0
        ),
    )


def swap(x, axes):
    return lax.all_to_all(x, axes, 0, 0, tiled=False)


def ahead(x, d):
    return lax.ppermute(x, "zh", [(i, i + d) for i in range(4 - d)])


def shards(queries, key_rows, values, out_grad, rate, rotation, refusal, proj_weight, proj_bias, positions):
    q, k, v, grad = queries[0], key_rows[0], values[0], out_grad[0]
    ref = refusal.T
    bias = jnp.pad(proj_bias, (0, 124))[None, :]
    rows = (BLOCK, WIDE)
    tile = (NPOS, 128)

    def space(shape, dtype=f32):
        return pltpu.VMEM(shape, dtype)

    def marks(*shape):
        return pltpu.SemaphoreType.DMA(shape)

    grad_state, small, logs, places = call(
        query_state,
        "ssaaaavvv",
        [((16, 96, 128), f32), ((24, 128), f32), ((8, 128), f32), (tile, jnp.int32)],
        [space(rows, bf16)] * 4 + [space((16, 96, 128)), marks(4), marks(2 * HEADS)],
        (0,),
        mib=60,
    )(rate, positions, q, k, grad, v, rotation, ref, proj_weight)
    later = swap(grad_state, NEAR)
    small = lax.psum(small, "head")
    moved, state, basis = call(
        key_state,
        "vvvvvvvvv",
        [(rows, bf16), ((16, 64, 128), f32), ((HEADS, 16, 128), f32)],
        [space((16, 64, 128)), marks(HEADS)],
        (1,),
    )(logs, places, small, v, k, rotation, ref, proj_weight, bias)
    state, later = lax.optimization_barrier((state, later))
    earlier = swap(state, NEAR)
    (own,) = call(backward_totals, "vv", [((96, 128), f32)], [space(tile)])(logs, later)
    groups = lax.all_gather(own, "zh")
    groups, earlier = lax.optimization_barrier((groups, earlier))
    (total,) = call(forward_totals, "vv", [((64, 128), f32)])(logs, earlier)
    passed = [ahead(total, d) for d in (2, 1, 3)]
    one, two, three = passed[1], passed[0], passed[2]
    (leaving,) = call(
        backward_carried,
        "vvvv",
        [((16, 88, 128), f32)],
        [space((16, 88, 128)), space(tile), marks(4)],
        (0,),
    )(logs, later, groups, basis)
    leaving, total = lax.optimization_barrier((leaving, total))
    leaving = swap(leaving, NEAR)
    (entering,) = call(
        forward_carried,
        "vvvvv",
        [((16, 64, 128), f32)],
        [space((16, 64, 128)), marks(4)],
        (0,),
    )(logs, earlier, one, two, three)
    (head_sums,) = call(sum_slices, "v", [(tile, f32)])(leaving)
    head_sums = lax.psum(head_sums, "head")
    entering = swap(entering, NEAR)
    (parts,) = call(products, "vvv", [((72, 128), f32)])(head_sums, bias, leaving)
    others = lax.ppermute(parts, "dp", [(0, 1), (1, 0)])
    attended_in, grad_q_in, grad_k, grad_v = call(
        backward_rest,
        "v" * 9,
        [(rows, f32)] * 2 + [(rows, bf16)] * 2,
        [space(rows, bf16)] * 2 + [marks(4, 2)],
        (2, 3),
    )(logs, places, q, k, moved, grad, leaving, basis, head_sums)
    attended, grad_q, grad_rotation, grad_weight, grad_bias = call(
        forward_rest,
        "vvvvvvvvvv",
        [(rows, bf16)] * 2 + [((4, WIDE), f32)] * 2 + [((4,), f32)],
        [space(rows, bf16)] * 2 + [marks(4, 2)],
        (0, 1),
    )(logs, q, grad, entering, attended_in, grad_q_in, small, ref, parts, others)
    return (
        attended[None],
        grad_q[None],
        grad_k[None],
        grad_v[None],
        grad_rotation,
        grad_weight,
        grad_bias,
    )


def solution(mesh):
    own = Mesh(mesh.devices.reshape(4, 4, 4, 4, 2), ("zh", "zl", "y", "head", "dp"))
    seq = ("zh", "zl", "y")
    stream = P("dp", seq, "head")
    return jax.shard_map(
        shards,
        mesh=own,
        in_specs=(
            stream,
            stream,
            stream,
            stream,
            P("head"),
            P(None, "head"),
            P("head", None),
            P(None, "head"),
            P(),
            P("dp", None),
        ),
        out_specs=(stream, stream, stream, stream, P(None, "head"), P(None, "head"), P()),
        check_vma=False,
    )
```
